256 devices in a mesh: kv: 32 (over z, x), req: 8 (over y, core).
Axes of the slice: x: 4, y: 4, z: 8, core: 2. Of those that a mesh axis runs over, the one named last changes fastest.
Arguments:
- hidden: bfloat16 [256, 8192], P('req', 'kv'), may hold values from -6 to 6
- q_weight: bfloat16 [8192, 8192], P('kv'), may hold values from -0.0625 to 0.0625
- new_key: bfloat16 [256, 1024], P('req'), may hold values from -6 to 6
- new_value: bfloat16 [256, 1024], P('req'), may hold values from -6 to 6
- key_cache: bfloat16 [8, 131072, 128], P('req', 'kv')
- value_cache: bfloat16 [8, 131072, 128], P('req', 'kv'), may hold values from -6 to 6
- req_doc: int32 [256], replicated, may hold values from 0 to 23
- doc_len: int32 [24], replicated, may hold values from 1 to 32768, as said below
- slot_doc: int32 [256], P('kv'), may hold values from 0 to 23, as said below
- slot_blk: int32 [256], P('kv'), may hold values from 0 to 63
Outputs:
- attended: bfloat16 [256, 8192], P('req')
The draws below stay inside these ranges and needn't reach their ends.
Inputs may be any that keep to these rules, and one draw needn't show every extreme that they name: `slot_doc`: every document has at least one slot, and exactly one document has 64 slots, the most; the slots of a document hold its blocks 0, 1, 2, ... once each, in no particular places. `doc_len`: A document with k slots has more than (k - 1) * 512 and at most k * 512 tokens; the document with the most slots fills its last block.
All inputs are finite; a program needn't handle non-finite values.
Results may differ from the reference program's by a relative error of at most 0.017.
Values may be sent and summed in bfloat16 or wider, within the bound.
No kernel may reach another device: no remote copies, remote signals or barrier semaphores. Data moves between devices by JAX's collectives and lax.ppermute only.
A program may use at most 128 MiB of HBM per device.

```python
import math
import jax
import jax.numpy as jnp
import numpy as np
from jax import lax

D = 8192
HQ = 64
GROUPS = 8
HD = 128
QPG = 8
BLOCK = 512
DOCS = 24
REQS = 256
TOTAL_SLOTS = 256
TOKENS = 131072


def layout(key):
    longest_length = TOTAL_SLOTS // 4
    remaining_blocks = TOTAL_SLOTS - longest_length
    cuts = jnp.sort(jax.random.permutation(key, remaining_blocks - 1)[:DOCS - 2] + 1).astype(jnp.int32)
    lows = jnp.concatenate([jnp.zeros((1,), jnp.int32), cuts])
    highs = jnp.concatenate([cuts, jnp.full((1,), remaining_blocks, jnp.int32)])
    others = (highs - lows).astype(jnp.int32)
    chosen = jax.random.randint(jax.random.fold_in(key, 5), (), 0, DOCS).astype(jnp.int32)
    rank = jnp.arange(DOCS).astype(jnp.int32)
    before = others[jnp.clip(rank, 0, DOCS - 2)]
    after = others[jnp.clip(rank - 1, 0, DOCS - 2)]
    sizes = jnp.where(rank < chosen, before, jnp.where(rank == chosen, longest_length, after)).astype(jnp.int32)
    ends = jnp.cumsum(sizes).astype(jnp.int32)
    starts = (ends - sizes).astype(jnp.int32)
    block_list = jnp.arange(TOTAL_SLOTS).astype(jnp.int32)
    owner = jnp.sum((block_list[:, None] >= ends[None, :DOCS - 1]).astype(jnp.int32), axis=1).astype(jnp.int32)
    within = (block_list - starts[owner]).astype(jnp.int32)
    sorted_index = jax.random.permutation(jax.random.fold_in(key, 7), TOTAL_SLOTS)
    return (owner[sorted_index], within[sorted_index], sizes, rank == chosen)


def draw_slot_doc(key, part):
    shared = layout(key)
    return shared[0].astype(jnp.int32)


def draw_slot_blk(key, part):
    shared = layout(key)
    return shared[1].astype(jnp.int32)


def draw_doc_len(key, part):
    shared = layout(key)
    key = jax.random.fold_in(key, 17)
    tail = jax.random.randint(key, (DOCS,), 1, BLOCK + 1).astype(jnp.int32)
    tail = jnp.where(shared[3], BLOCK, tail)
    return ((shared[2] - 1) * BLOCK + tail).astype(jnp.int32)


def draw_key_cache(key, part):
    key = jax.random.fold_in(key, 19)
    base = jax.random.normal(key, (GROUPS, TOKENS, HD), jnp.float32)
    base = jnp.clip(base, -6.0, 6.0)
    return base.astype(jnp.bfloat16)


def set_ends(array, rng, smallest, top_value):
    extent = array.shape
    place = [jax.random.randint(jax.random.fold_in(rng, axis), (), 0, extent[axis]) for axis in range(len(extent))]
    array = array.at[tuple(place)].set(smallest)
    longest = extent.index(max(extent))
    place[longest] = (place[longest] + 1) % extent[longest]
    return array.at[tuple(place)].set(top_value)


def steps_of(key, dims, pieces, least, largest):
    def one(position, blocks):
        draws = jax.random.uniform(jax.random.fold_in(jax.random.fold_in(key, 6), position), (blocks,), jnp.float32, least / len(pieces), largest / len(pieces))
        return jnp.repeat(jnp.exp(draws), dims[position] // blocks).reshape((-1,) + (1,) * (len(dims) - position - 1))

    factor_of = one(*pieces[0])
    for cut in pieces[1:]:
        factor_of = factor_of * one(*cut)
    return factor_of


def rank_bounds(count, lean):
    weights = [(1 << 20) // math.isqrt(standing ** lean) + 1 for standing in range(1, count + 1)]
    scale = 1 + sum(weights) // (1 << 30)
    return np.cumsum(np.array([max(1, weight // scale) for weight in weights]))


def ranked_ids(stream_key, extent, number_of, skew):
    listing = rank_bounds(number_of, skew)
    lot = jax.random.randint(jax.random.fold_in(stream_key, 1), extent, 0, int(listing[number_of - 1]))
    grade = jnp.searchsorted(jnp.asarray(listing, jnp.int32), lot, side="right")
    return jax.random.permutation(jax.random.fold_in(stream_key, 2), number_of)[grade].astype(jnp.int32)


def noise(key, dims, scale, limit, shards=(), held_as=jnp.bfloat16):
    entries = jax.random.normal(key, dims, jnp.float32) * scale
    if len(shards) > 0:
        entries = steps_of(key, dims, shards, -0.22, 0.18) * entries
    return jnp.clip(entries, min=-limit, max=limit).astype(held_as)


def setup_inputs(seed: int = 0) -> dict:
    key_list = jax.random.split(jax.random.key(seed), 11)
    return {
        "hidden": noise(key_list[0], (REQS, D), 1.0, 6.0, ((0, 8), (1, 32))),
        "q_weight": noise(key_list[1], (D, HQ * HD), D ** -0.5, 0.0625, ((0, 32),)),
        "new_key": noise(key_list[2], (REQS, GROUPS * HD), 1.0, 6.0, ((0, 8),)),
        "new_value": noise(key_list[3], (REQS, GROUPS * HD), 1.0, 6.0, ((0, 8),)),
        "key_cache": draw_key_cache(jax.random.fold_in(key_list[10], 71), 0),
        "value_cache": noise(key_list[5], (GROUPS, TOKENS, HD), 1.0, 6.0, ((0, 8), (1, 32))),
        "req_doc": set_ends(ranked_ids(key_list[6], (REQS,), DOCS, 2), jax.random.fold_in(key_list[6], 3), 0, DOCS - 1).astype(jnp.int32),
        "doc_len": draw_doc_len(jax.random.fold_in(key_list[10], 71), 0),
        "slot_doc": draw_slot_doc(jax.random.fold_in(key_list[10], 71), 0),
        "slot_blk": draw_slot_blk(jax.random.fold_in(key_list[10], 71), 0),
    }


NEG = -1e30


def reference(hidden, q_weight, new_key, new_value, key_cache, value_cache, req_doc, doc_len, slot_doc, slot_blk):
    scale = HD ** -0.5
    query = jnp.dot(hidden, q_weight, preferred_element_type=jnp.float32).astype(jnp.bfloat16)
    heads = query.astype(jnp.float32).reshape(REQS, GROUPS, QPG, HD)
    own_key = new_key.astype(jnp.float32).reshape(REQS, GROUPS, 1, HD)
    own_val = new_value.astype(jnp.float32).reshape(REQS, GROUPS, 1, HD)
    top = jnp.sum(heads * own_key, axis=-1) * scale
    total = jnp.ones((REQS, GROUPS, QPG), jnp.float32)
    weighted = jnp.broadcast_to(own_val, (REQS, GROUPS, QPG, HD)).astype(jnp.float32)
    doc_ids = jnp.arange(DOCS).astype(jnp.int32)
    slot_len = jnp.sum(jnp.where(slot_doc[:, None] == doc_ids[None, :], doc_len[None, :], 0), axis=1)
    remain = jnp.clip(slot_len - slot_blk * BLOCK, 0, BLOCK)
    live = (jnp.arange(BLOCK).astype(jnp.int32)[None, :] < remain[:, None]).reshape(-1)
    token_document = jnp.repeat(slot_doc, BLOCK)
    width = 4 * BLOCK

    def step(carry, index):
        top, total, weighted = carry
        start = (index * width).astype(jnp.int32)
        keys = lax.dynamic_slice_in_dim(key_cache, start, width, 1).astype(jnp.float32)
        vals = lax.dynamic_slice_in_dim(value_cache, start, width, 1).astype(jnp.float32)
        docs = lax.dynamic_slice_in_dim(token_document, start, width, 0)
        alive = lax.dynamic_slice_in_dim(live, start, width, 0)
        match = ((req_doc[:, None] == docs[None, :]) & alive[None, :])[:, None, None, :]
        scores = jnp.einsum('rgjd,gtd->rgjt', heads, keys) * scale
        updated_maximum = jnp.maximum(top, jnp.max(jnp.where(match, scores, NEG), axis=-1))
        probs = jnp.where(match, jnp.exp(scores - updated_maximum[..., None]), 0.0)
        shrink = jnp.exp(top - updated_maximum)
        total = total * shrink + jnp.sum(probs, axis=-1)
        rounded = lax.optimization_barrier(probs.astype(jnp.bfloat16)).astype(jnp.float32)
        weighted = weighted * shrink[..., None] + jnp.einsum('rgjt,gtd->rgjd', rounded, vals)
        return (updated_maximum, total, weighted), None

    decode_rounds = jnp.arange(TOTAL_SLOTS // 4).astype(jnp.int32)
    (top, total, weighted), unused = lax.scan(step, (top, total, weighted), decode_rounds)
    return (weighted / total[..., None]).reshape(REQS, HQ * HD).astype(jnp.bfloat16)
```

```python
import functools

import jax
import jax.numpy as jnp
from jax import lax
from jax.experimental import pallas as pl
from jax.experimental.pallas import tpu as pltpu
from jax.sharding import PartitionSpec as P

HD = 128
QPG = 8
BLOCK = 512
DOCS = 24
CHUNK = 16
ROWS = CHUNK * QPG

NEG = -1e30
F32 = jnp.float32
BF16 = jnp.bfloat16


def dot(a, b):
    return jnp.dot(a, b, preferred_element_type=F32)


def iota(shape, axis):
    return lax.broadcasted_iota(jnp.int32, shape, axis)


def vmem():
    return pl.BlockSpec(memory_space=pltpu.VMEM)


def smem():
    return pl.BlockSpec(memory_space=pltpu.SMEM)


def pack_kernel(place_ref, hidden_ref, key_ref, value_ref, out_ref):
    owners = out_ref.shape[0]
    rows = hidden_ref.shape[0]
    pick = jnp.where(iota((8, rows), 1) == place_ref[0], 1.0, 0.0).astype(BF16)
    key = dot(pick, key_ref[...]).astype(BF16)
    value = dot(pick, value_ref[...]).astype(BF16)
    for i in range(owners):
        out_ref[i, :rows, :] = hidden_ref[...]
        out_ref[i, rows:, :HD] = key[:, i * HD : (i + 1) * HD]
        out_ref[i, rows:, HD:] = value[:, i * HD : (i + 1) * HD]


def project_kernel(place_ref, packed_ref, weight_ref, out_ref):
    owners, padded, depth = packed_ref.shape
    rows = padded - 8
    count = owners * rows
    row = iota((count, count), 0)
    order = (row % owners) * rows + row // owners
    pick = jnp.where(iota((count, count), 1) == order, 1.0, 0.0).astype(BF16)
    hidden = packed_ref[:, :rows, :].reshape(count, depth)
    hidden = dot(pick, hidden).astype(BF16)
    out_ref[...] = dot(hidden, weight_ref[...])


def attend_kernel(meta_ref, doc_col_ref, doc_row_ref, query_ref, key_ref, value_ref, out_ref,
                  q_ref, d_ref, m_ref, l_ref, acc_ref):
    count = query_ref.shape[0]
    chunks = count // CHUNK
    slots = key_ref.shape[0] // BLOCK
    scale = HD ** (-0.5)
    col = doc_col_ref[:, :1]
    row = doc_row_ref[:1, :]
    down, across = iota((count, count), 0), iota((count, count), 1)
    before = jnp.where((col < row) | ((col == row) & (down < across)), 1.0, 0.0)
    rank_row = jnp.sum(before, axis=0, keepdims=True).astype(jnp.int32)
    behind = jnp.where((row < col) | ((row == col) & (across < down)), 1.0, 0.0)
    rank_col = jnp.sum(behind, axis=1, keepdims=True).astype(jnp.int32)
    sort = jnp.where(down == rank_row, 1.0, 0.0).astype(BF16)
    unsort = jnp.where(across == rank_col, 1.0, 0.0).astype(BF16)
    ordered = dot(sort, query_ref[...]).astype(BF16)
    docs = dot(sort, doc_col_ref[...].astype(F32).astype(BF16))
    for c in range(chunks):
        for h in range(QPG):
            at = c * ROWS + h * CHUNK
            q_ref[at : at + CHUNK, :] = ordered[c * CHUNK : (c + 1) * CHUNK, h * HD : (h + 1) * HD]
            d_ref[at : at + CHUNK, :] = docs[c * CHUNK : (c + 1) * CHUNK, :]
    m_ref[...] = jnp.full_like(m_ref, NEG)
    l_ref[...] = jnp.zeros_like(l_ref)
    acc_ref[...] = jnp.zeros_like(acc_ref)

    def slot(s, _):
        doc = meta_ref[s]
        start = pl.multiple_of(s * BLOCK, BLOCK)
        keys = key_ref[pl.ds(start, BLOCK), :]
        values = value_ref[pl.ds(start, BLOCK), :]
        alive = iota((ROWS, BLOCK), 1) < meta_ref[3 * slots + s]

        def chunk(c, _):
            here = pl.ds(pl.multiple_of(c * ROWS, ROWS), ROWS)
            scores = lax.dot_general(
                q_ref[here, :], keys, (((1,), (1,)), ((), ())), preferred_element_type=F32
            ) * scale
            match = (d_ref[here, :1] == doc.astype(F32)) & alive
            scores = jnp.where(match, scores, NEG)
            old = m_ref[here, :]
            top = jnp.maximum(old, jnp.max(scores, axis=1, keepdims=True))
            probs = jnp.where(match, jnp.exp(scores - top[:, :1]), 0.0)
            shrink = jnp.exp(old - top)
            m_ref[here, :] = top
            l_ref[here, :] = l_ref[here, :] * shrink + jnp.sum(probs, axis=1, keepdims=True)
            acc_ref[here, :] = acc_ref[here, :] * shrink + dot(probs.astype(BF16), values)
            return 0

        lax.fori_loop(meta_ref[slots + s], meta_ref[2 * slots + s], chunk, 0)
        return 0

    lax.fori_loop(0, slots, slot, 0)

    lane = iota((CHUNK, HD), 1)
    total, facts = [], []
    for c in range(chunks):
        pieces = jnp.zeros((CHUNK, HD), F32)
        heads = []
        for h in range(QPG):
            here = pl.ds(c * ROWS + h * CHUNK, CHUNK)
            heads.append(acc_ref[here, :].astype(BF16))
            at = h
            for rest in (m_ref[here, :], l_ref[here, :]):
                for _ in range(3):
                    part = rest.astype(BF16).astype(F32)
                    rest = rest - part
                    pieces = jnp.where(lane == at, part, pieces)
                    at += QPG
        total.append(jnp.concatenate(heads, axis=1))
        facts.append(pieces.astype(BF16))
    out_ref[:, : QPG * HD] = dot(unsort, jnp.concatenate(total, axis=0)).astype(BF16)
    out_ref[:, QPG * HD :] = dot(unsort, jnp.concatenate(facts, axis=0)).astype(BF16)


def combine_kernel(parts_ref, query_ref, own_ref, out_ref):
    sources, owners, _ = parts_ref.shape
    wide = QPG * HD
    facts = parts_ref[:, :, wide:].reshape(sources * owners, HD)
    place, head = iota((HD, wide), 0), iota((HD, wide), 1) // HD
    pick_m = jnp.where((place % QPG == head) & (place < 3 * QPG), 1.0, 0.0).astype(BF16)
    pick_l = jnp.where(
        (place % QPG == head) & (place >= 3 * QPG) & (place < 6 * QPG), 1.0, 0.0
    ).astype(BF16)
    tops = dot(facts, pick_m).reshape(sources, owners, wide)
    totals = dot(facts, pick_l).reshape(sources, owners, wide)
    query = query_ref[...].astype(F32)
    own_key = own_ref[:, :HD].astype(F32)
    own_value = own_ref[:, HD:].astype(F32)
    own = jnp.concatenate(
        [
            jnp.broadcast_to(
                jnp.sum(query[:, h * HD : (h + 1) * HD] * own_key, axis=1, keepdims=True),
                (owners, HD),
            )
            for h in range(QPG)
        ],
        axis=1,
    ) * (HD ** (-0.5))
    top = jnp.maximum(own, jnp.max(tops, axis=0))
    weight = jnp.exp(own - top)
    total = weight
    mixed = weight * jnp.concatenate([own_value] * QPG, axis=1)
    weights = jnp.exp(tops - top[None])
    total = total + jnp.sum(weights * totals, axis=0)
    mixed = mixed + jnp.sum(weights * parts_ref[:, :, :wide].astype(F32), axis=0)
    out_ref[...] = (mixed / total).astype(BF16)


def per_device(
    hidden,
    q_weight,
    new_key,
    new_value,
    key_cache,
    value_cache,
    req_doc,
    doc_len,
    slot_doc,
    slot_blk,
):
    owners, sources = lax.axis_size("req"), lax.axis_size("kv")
    rows, depth = hidden.shape
    count = owners * rows
    wide = QPG * HD
    slots = slot_doc.shape[0]
    mine = lax.axis_index("req").reshape(1)
    place = lax.axis_index("kv").reshape(1)

    docs = req_doc.reshape(owners, rows).T.reshape(count)
    lower = jnp.sum((docs[None, :] < slot_doc[:, None]).astype(jnp.int32), axis=1)
    upper = jnp.sum((docs[None, :] <= slot_doc[:, None]).astype(jnp.int32), axis=1)
    doc_ids = jnp.arange(DOCS)
    slot_len = jnp.sum(
        jnp.where(slot_doc[:, None] == doc_ids[None, :], doc_len[None, :], 0), axis=1
    )
    remain = jnp.clip(slot_len - slot_blk * BLOCK, 0, BLOCK)
    first = lower // CHUNK
    last = jnp.where(upper > lower, (upper + CHUNK - 1) // CHUNK, first)
    meta = jnp.concatenate([slot_doc, first, last, remain])
    doc_col = jnp.broadcast_to(docs[:, None], (count, HD))
    doc_row = jnp.broadcast_to(docs[None, :], (8, count))

    packed = pl.pallas_call(
        pack_kernel,
        out_shape=jax.ShapeDtypeStruct((owners, rows + 8, depth), BF16),
        in_specs=[smem(), vmem(), vmem(), vmem()],
        out_specs=vmem(),
    )(place, hidden, new_key, new_value)
    packed = lax.all_to_all(packed, "req", 0, 0, tiled=True)
    partial = pl.pallas_call(
        project_kernel,
        out_shape=jax.ShapeDtypeStruct((count, wide), F32),
        grid_spec=pltpu.PrefetchScalarGridSpec(
            num_scalar_prefetch=1,
            grid=(1,),
            in_specs=[
                pl.BlockSpec((owners, rows + 8, depth), lambda g, at: (0, 0, 0)),
                pl.BlockSpec((depth, wide), lambda g, at: (0, at[0])),
            ],
            out_specs=pl.BlockSpec((count, wide), lambda g, at: (0, 0)),
        ),
    )(mine, packed, q_weight)
    partial = lax.all_to_all(partial.astype(jnp.float16), "kv", 0, 0, tiled=True)
    query = jnp.sum(partial.reshape(sources, owners, wide).astype(F32), axis=0).astype(BF16)
    every = lax.all_to_all(
        jnp.broadcast_to(query[None], (sources, owners, wide)), "kv", 0, 0, tiled=True
    ).reshape(count, wide)
    parts = pl.pallas_call(
        attend_kernel,
        out_shape=jax.ShapeDtypeStruct((count, wide + HD), BF16),
        in_specs=[smem()] + [vmem()] * 5,
        out_specs=vmem(),
        scratch_shapes=[
            pltpu.VMEM((count * QPG, HD), BF16),
            pltpu.VMEM((count * QPG, HD), F32),
            pltpu.VMEM((count * QPG, HD), F32),
            pltpu.VMEM((count * QPG, HD), F32),
            pltpu.VMEM((count * QPG, HD), F32),
        ],
        compiler_params=pltpu.CompilerParams(vmem_limit_bytes=40 * 1024 * 1024),
    )(meta, doc_col, doc_row, every, key_cache[0], value_cache[0])
    parts = lax.all_to_all(parts, "kv", 0, 0, tiled=True).reshape(sources, owners, wide + HD)
    result = pl.pallas_call(
        combine_kernel,
        out_shape=jax.ShapeDtypeStruct((owners, wide), BF16),
        in_specs=[vmem()] * 3,
        out_specs=vmem(),
        compiler_params=pltpu.CompilerParams(vmem_limit_bytes=40 * 1024 * 1024),
    )(parts, query, packed[:, rows, :])
    result = lax.all_to_all(result, "req", 0, 0, tiled=True)
    result = lax.all_to_all(
        jnp.broadcast_to(result[None], (sources, owners, wide)), "kv", 0, 0, tiled=True
    )
    return result.reshape(rows, owners * wide)


def solution(mesh):
    return jax.shard_map(
        per_device,
        mesh=mesh,
        in_specs=(
            P("req", "kv"),
            P("kv", None),
            P("req", None),
            P("req", None),
            P("req", "kv", None),
            P("req", "kv", None),
            P(),
            P(),
            P("kv"),
            P("kv"),
        ),
        out_specs=P("req", None),
        check_vma=False,
    )
```

```python
import jax
import jax.numpy as jnp
from jax import lax
from jax.experimental import pallas as pl
from jax.experimental.pallas import tpu as pltpu
from jax.sharding import Mesh
from jax.sharding import PartitionSpec as P

HD = 128
QPG = 8
BLOCK = 512
DOCS = 24
CHUNK = 16
ROWS = CHUNK * QPG
TOGETHER = 4
PIECES = 3

NEG = -1e30
F32 = jnp.float32
BF16 = jnp.bfloat16
VMEM_BYTES = 40 * 1024 * 1024


def dot(a, b):
    return jnp.dot(a, b, preferred_element_type=F32)


def iota(shape, axis):
    return lax.broadcasted_iota(jnp.int32, shape, axis)


def vmem():
    return pl.BlockSpec(memory_space=pltpu.VMEM)


def smem():
    return pl.BlockSpec(memory_space=pltpu.SMEM)


def split(value):
    pieces = []
    for _ in range(PIECES):
        piece = value.astype(BF16).astype(F32)
        pieces.append(piece)
        value = value - piece
    return pieces


def attend_kernel(
    meta_ref,
    doc_col_ref,
    doc_row_ref,
    query_ref,
    key_ref,
    value_ref,
    out_ref,
    list_ref,
    q_ref,
    d_ref,
    m_ref,
    l_ref,
    acc_ref,
):
    count = doc_col_ref.shape[0]
    chunks = count // CHUNK
    slots = key_ref.shape[0] // BLOCK
    quarters = out_ref.shape[0]
    here = count // quarters
    scale = HD ** (-0.5)

    found = 0
    for s in range(slots):

        def put(c, n, s=s):
            list_ref[n] = s * chunks + c
            return n + 1

        found = lax.fori_loop(meta_ref[slots + s], meta_ref[2 * slots + s], put, found)
    for u in range(TOGETHER):
        list_ref[found + u] = 0

    col = doc_col_ref[:, :1]
    row = doc_row_ref[:1, :]
    down, across = iota((count, count), 0), iota((count, count), 1)
    before = jnp.where((col < row) | ((col == row) & (down < across)), 1.0, 0.0)
    rank_row = jnp.sum(before, axis=0, keepdims=True).astype(jnp.int32)
    behind = jnp.where((row < col) | ((row == col) & (across < down)), 1.0, 0.0)
    rank_col = jnp.sum(behind, axis=1, keepdims=True).astype(jnp.int32)
    sort = jnp.where(down == rank_row, 1.0, 0.0).astype(BF16)
    unsort = jnp.where(across == rank_col, 1.0, 0.0).astype(BF16)
    docs = dot(sort, doc_col_ref[...].astype(F32).astype(BF16))
    for h in range(QPG):
        ordered = dot(sort, query_ref[h * count : (h + 1) * count, :]).astype(BF16)
        for c in range(chunks):
            at = c * ROWS + h * CHUNK
            q_ref[at : at + CHUNK, :] = ordered[c * CHUNK : (c + 1) * CHUNK, :]
            d_ref[at : at + CHUNK, :] = docs[c * CHUNK : (c + 1) * CHUNK, :]
    m_ref[...] = jnp.full_like(m_ref, NEG)
    l_ref[...] = jnp.zeros_like(l_ref)
    acc_ref[...] = jnp.zeros_like(acc_ref)

    def some(step, _):
        local = []
        for u in range(TOGETHER):
            k = step * TOGETHER + u
            s, c = list_ref[k] // chunks, list_ref[k] % chunks
            doc = jnp.where(k < found, meta_ref[s], -1).astype(F32)
            rows = pl.ds(pl.multiple_of(c * ROWS, ROWS), ROWS)
            tokens = pl.ds(pl.multiple_of(s * BLOCK, BLOCK), BLOCK)
            scores = lax.dot_general(
                q_ref[rows, :],
                key_ref[tokens, :],
                (((1,), (1,)), ((), ())),
                preferred_element_type=F32,
            )
            alive = iota((ROWS, BLOCK), 1) < meta_ref[3 * slots + s]
            scores = jnp.where(alive, scores * scale, NEG)
            top = jnp.max(scores, axis=1, keepdims=True)
            probs = jnp.exp(scores - top)
            total = jnp.sum(probs, axis=1, keepdims=True)
            mixed = dot(probs.astype(BF16), value_ref[tokens, :])
            local.append((rows, doc, top, total, mixed))
        for rows, doc, top, total, mixed in local:
            match = d_ref[rows, :] == doc
            old = m_ref[rows, :]
            new = jnp.maximum(old, top)
            left, right = jnp.exp(old - new), jnp.exp(top - new)
            m_ref[rows, :] = jnp.where(match, new, old)
            total_old, mixed_old = l_ref[rows, :], acc_ref[rows, :]
            l_ref[rows, :] = jnp.where(match, total_old * left + total * right, total_old)
            acc_ref[rows, :] = jnp.where(match, mixed_old * left + mixed * right, mixed_old)
        return 0

    lax.fori_loop(0, (found + TOGETHER - 1) // TOGETHER, some, 0)

    lane = iota((CHUNK, HD), 1)
    facts = []
    for c in range(chunks):
        fact = jnp.zeros((CHUNK, HD), F32)
        for h in range(QPG):
            at = c * ROWS + h * CHUNK
            fact = jnp.where(lane == h, m_ref[at : at + CHUNK, :], fact)
            fact = jnp.where(lane == QPG + h, l_ref[at : at + CHUNK, :], fact)
        facts.append(fact)
    pieces = split(jnp.concatenate(facts, axis=0))
    packed = pieces[0]
    for k in range(1, PIECES):
        packed = packed + pltpu.roll(pieces[k], 2 * QPG * k, 1)
    blocks = []
    for h in range(QPG):
        blocks.append(
            jnp.concatenate(
                [
                    acc_ref[c * ROWS + h * CHUNK : c * ROWS + (h + 1) * CHUNK, :]
                    for c in range(chunks)
                ],
                axis=0,
            )
        )
    blocks.append(packed)
    for h, block in enumerate(blocks):
        block = dot(unsort, block.astype(BF16)).astype(BF16)
        for x in range(quarters):
            out_ref[x, h, :, :] = block[x * here : (x + 1) * here, :]


def merge_kernel(place_ref, parts_ref, query_ref, out_ref):
    sources, _, here, _ = parts_ref.shape
    owners = here // 8
    wide = QPG * HD
    lanes, head = iota((HD, wide), 0), iota((HD, wide), 1) // HD
    known = lanes < 2 * QPG * PIECES
    pick_m = jnp.where((lanes % (2 * QPG) == head) & known, 1.0, 0.0).astype(BF16)
    pick_l = jnp.where((lanes % (2 * QPG) == head + QPG) & known, 1.0, 0.0).astype(BF16)
    facts = [parts_ref[s, QPG, :, :] for s in range(sources)]
    tops = [dot(fact, pick_m) for fact in facts]
    totals = [dot(fact, pick_l) for fact in facts]
    top = tops[0]
    for s in range(1, sources):
        top = jnp.maximum(top, tops[s])
    total = jnp.zeros((here, wide), F32)
    mixed = [jnp.zeros((here, HD), F32)] * QPG
    for s in range(sources):
        weight = jnp.exp(tops[s] - top)
        total = total + weight * totals[s]
        for h in range(QPG):
            part = parts_ref[s, h, :, :].astype(F32)
            mixed[h] = mixed[h] + weight[:, h * HD : (h + 1) * HD] * part
    lane = iota((here, HD), 1)
    z, x = place_ref[0], place_ref[1]
    base = (z + QPG // 2) % QPG * 16
    count = query_ref.shape[0] // QPG
    for h in range(QPG):
        at = pl.multiple_of(h * count + x * here, here)
        query = query_ref[pl.ds(at, here), :].astype(F32)
        fact = jnp.where(lane // 16 == z, query, 0.0)
        pieces = split(top[:, h * HD : (h + 1) * HD]) + split(total[:, h * HD : (h + 1) * HD])
        for k, piece in enumerate(pieces):
            fact = jnp.where(lane == base + k, piece, fact)
        for i in range(owners):
            rows = slice(8 * i, 8 * i + 8)
            tile = jnp.concatenate([mixed[h][rows], fact[rows]], axis=0)
            out_ref[i * QPG + h, :, :] = tile.astype(BF16)


def finish_kernel(place_ref, parts_ref, key_ref, value_ref, out_ref):
    owners = parts_ref.shape[0] // QPG
    rows = key_ref.shape[0]
    x = place_ref[1]
    pick = jnp.where(iota((8, rows), 1) == iota((8, rows), 0) + 8 * x, 1.0, 0.0).astype(BF16)
    own_key, own_value = dot(pick, key_ref[...]), dot(pick, value_ref[...])
    lanes, column = iota((HD, 2 * HD), 0), iota((HD, 2 * HD), 1)
    lane = iota((8, HD), 1)
    spread = []
    for z in range(QPG):
        base = (z + QPG // 2) % QPG * 16
        low = jnp.where(column < HD, base, base + PIECES)
        pick = jnp.where((lanes >= low) & (lanes < low + PIECES), 1.0, 0.0).astype(BF16)
        fact = jnp.concatenate(
            [parts_ref[i * QPG + z, :, :].astype(F32)[8:] for i in range(owners)], axis=0
        )
        spread.append((dot(fact.astype(BF16), pick), fact))
    outs = []
    for i in range(owners):
        at, wide = slice(8 * i, 8 * i + 8), slice(i * HD, (i + 1) * HD)
        query = jnp.zeros((8, HD), F32)
        for z in range(QPG):
            query = jnp.where(lane // 16 == z, spread[z][1][at], query)
        own = jnp.sum(query * own_key[:, wide], axis=1, keepdims=True) * (HD ** (-0.5))
        own = jnp.broadcast_to(own, (8, HD))
        top = own
        for z in range(QPG):
            top = jnp.maximum(top, spread[z][0][at, :HD])
        total = jnp.exp(own - top)
        mixed = total * own_value[:, wide]
        for z in range(QPG):
            weight = jnp.exp(spread[z][0][at, :HD] - top)
            total = total + weight * spread[z][0][at, HD:]
            mixed = mixed + weight * parts_ref[i * QPG + z, :, :].astype(F32)[:8]
        outs.append(mixed / total)
    done = jnp.concatenate(outs, axis=0).astype(BF16)
    for k in range(out_ref.shape[0]):
        out_ref[k, :, :] = done


def per_device(
    hidden,
    q_weight,
    new_key,
    new_value,
    key_cache,
    value_cache,
    req_doc,
    doc_len,
    slot_doc,
    slot_blk,
):
    depths, quarters = lax.axis_size("z"), lax.axis_size("x")
    owners = lax.axis_size("y") * lax.axis_size("c")
    sources = depths * quarters
    rows = hidden.shape[0]
    count = owners * rows
    here = count // quarters
    slots = slot_doc.shape[0]
    place = jnp.stack([lax.axis_index("z"), lax.axis_index("x")])

    docs = req_doc.reshape(owners, quarters, rows // quarters).transpose(1, 0, 2).reshape(count)
    lower = jnp.sum((docs[None, :] < slot_doc[:, None]).astype(jnp.int32), axis=1)
    upper = jnp.sum((docs[None, :] <= slot_doc[:, None]).astype(jnp.int32), axis=1)
    doc_ids = jnp.arange(DOCS)
    slot_len = jnp.sum(
        jnp.where(slot_doc[:, None] == doc_ids[None, :], doc_len[None, :], 0), axis=1
    )
    remain = jnp.clip(slot_len - slot_blk * BLOCK, 0, BLOCK)
    first = lower // CHUNK
    last = jnp.where((upper > lower) & (remain > 0), (upper + CHUNK - 1) // CHUNK, first)
    meta = jnp.concatenate([slot_doc, first, last, remain])
    doc_col = jnp.broadcast_to(docs[:, None], (count, HD))
    doc_row = jnp.broadcast_to(docs[None, :], (8, count))

    partial = dot(hidden, q_weight).astype(jnp.float16)
    partial = lax.all_to_all(partial, "x", 0, 0, tiled=True)
    partial = jnp.sum(partial.reshape(quarters, rows // quarters, -1).astype(F32), axis=0)
    partial = partial.astype(jnp.float16).reshape(8, owners * QPG, HD).transpose(1, 0, 2)
    partial = lax.all_to_all(partial, ("y", "c", "z"), 0, 0, tiled=True)
    query = jnp.sum(partial.reshape(owners, depths, 8, HD).astype(F32), axis=1).astype(BF16)
    every = lax.all_to_all(
        jnp.broadcast_to(query.reshape(1, here, HD), (sources, here, HD)),
        ("z", "x"),
        0,
        0,
        tiled=True,
    ).reshape(QPG * count, HD)
    params = pltpu.CompilerParams(vmem_limit_bytes=VMEM_BYTES)
    parts = pl.pallas_call(
        attend_kernel,
        out_shape=jax.ShapeDtypeStruct((quarters, QPG + 1, here, HD), BF16),
        in_specs=[smem()] + [vmem()] * 5,
        out_specs=vmem(),
        scratch_shapes=[
            pltpu.SMEM((slots * (count // CHUNK) + TOGETHER,), jnp.int32),
            pltpu.VMEM((count * QPG, HD), BF16),
            pltpu.VMEM((count * QPG, HD), F32),
            pltpu.VMEM((count * QPG, HD), F32),
            pltpu.VMEM((count * QPG, HD), F32),
            pltpu.VMEM((count * QPG, HD), F32),
        ],
        compiler_params=params,
    )(meta, doc_col, doc_row, every, key_cache[0], value_cache[0])
    parts = lax.all_to_all(parts, "x", 0, 0, tiled=True)
    parts = pl.pallas_call(
        merge_kernel,
        out_shape=jax.ShapeDtypeStruct((owners * QPG, 16, HD), BF16),
        in_specs=[smem(), vmem(), vmem()],
        out_specs=vmem(),
        compiler_params=params,
    )(place, parts, every)
    parts = lax.all_to_all(parts, ("y", "c", "z"), 0, 0, tiled=True)
    result = pl.pallas_call(
        finish_kernel,
        out_shape=jax.ShapeDtypeStruct((sources, here, HD), BF16),
        in_specs=[smem(), vmem(), vmem(), vmem()],
        out_specs=vmem(),
        compiler_params=params,
    )(place, parts, new_key, new_value)
    result = lax.all_to_all(result, ("z", "x"), 0, 0, tiled=True)
    result = result.reshape(depths, quarters, owners, 8, HD).transpose(1, 3, 2, 0, 4)
    return result.reshape(rows, owners * QPG * HD)


def solution(mesh):
    sizes = (8, 4, 4, 2)
    mesh = Mesh(mesh.devices.reshape(sizes), ("z", "x", "y", "c"))
    kv, req = ("z", "x"), ("y", "c")
    return jax.shard_map(
        per_device,
        mesh=mesh,
        in_specs=(
            P(req, kv),
            P(kv, None),
            P(req, None),
            P(req, None),
            P(req, kv, None),
            P(req, kv, None),
            P(),
            P(),
            P(kv),
            P(kv),
        ),
        out_specs=P(req, None),
        check_vma=False,
    )
```

```python
import jax
import jax.numpy as jnp
from jax import lax
from jax.experimental import pallas as pl
from jax.experimental.pallas import tpu as pltpu
from jax.sharding import Mesh
from jax.sharding import PartitionSpec as P

HD = 128
QPG = 8
BLOCK = 512
DOCS = 24
CHUNK = 16
ROWS = CHUNK * QPG
TOGETHER = 4
PIECES = 3

NEG = -1e30
F32 = jnp.float32
BF16 = jnp.bfloat16
VMEM_BYTES = 40 * 1024 * 1024


def dot(a, b):
    return jnp.dot(a, b, preferred_element_type=F32)


def iota(shape, axis):
    return lax.broadcasted_iota(jnp.int32, shape, axis)


def vmem():
    return pl.BlockSpec(memory_space=pltpu.VMEM)


def smem():
    return pl.BlockSpec(memory_space=pltpu.SMEM)


def split(value):
    pieces = []
    for _ in range(PIECES):
        piece = value.astype(BF16).astype(F32)
        pieces.append(piece)
        value = value - piece
    return pieces


def attend_kernel(meta_ref, doc_col_ref, doc_row_ref, *refs):
    quarters = (len(refs) - 8) // 2
    query_refs, (key_ref, value_ref) = refs[:quarters], refs[quarters : quarters + 2]
    out_refs = refs[quarters + 2 : 2 * quarters + 2]
    list_ref, q_ref, d_ref, m_ref, l_ref, acc_ref = refs[2 * quarters + 2 :]
    count = doc_col_ref.shape[0]
    chunks = count // CHUNK
    slots = key_ref.shape[0] // BLOCK
    here = count // quarters
    scale = HD ** (-0.5)

    found = 0
    for s in range(slots):

        def put(c, n, s=s):
            list_ref[n] = s * chunks + c
            return n + 1

        found = lax.fori_loop(meta_ref[slots + s], meta_ref[2 * slots + s], put, found)
    for u in range(TOGETHER):
        list_ref[found + u] = 0

    col = doc_col_ref[:, :1]
    row = doc_row_ref[:1, :]
    down, across = iota((count, count), 0), iota((count, count), 1)
    before = jnp.where((col < row) | ((col == row) & (down < across)), 1.0, 0.0)
    rank_row = jnp.sum(before, axis=0, keepdims=True).astype(jnp.int32)
    behind = jnp.where((row < col) | ((row == col) & (across < down)), 1.0, 0.0)
    rank_col = jnp.sum(behind, axis=1, keepdims=True).astype(jnp.int32)
    sort = jnp.where(down == rank_row, 1.0, 0.0).astype(BF16)
    unsort = jnp.where(across == rank_col, 1.0, 0.0).astype(BF16)
    docs = dot(doc_row_ref[...].astype(F32).astype(BF16), unsort)
    docs = jnp.concatenate([docs] * (chunks // 8), axis=0)
    docs = jnp.where(iota((chunks, count), 1) // CHUNK == iota((chunks, count), 0), docs, 0.0)
    same = iota((count, ROWS), 0) % CHUNK == iota((count, ROWS), 1) % CHUNK
    d_ref[...] = dot(docs.astype(BF16), jnp.where(same, 1.0, 0.0).astype(BF16))
    for h in range(QPG):
        blocks = jnp.concatenate([ref[h, :, :] for ref in query_refs], axis=0)
        ordered = dot(sort, blocks).astype(BF16)
        for c in range(chunks):
            at = c * ROWS + h * CHUNK
            q_ref[at : at + CHUNK, :] = ordered[c * CHUNK : (c + 1) * CHUNK, :]
    m_ref[...] = jnp.full_like(m_ref, NEG)
    l_ref[...] = jnp.zeros_like(l_ref)
    acc_ref[...] = jnp.zeros_like(acc_ref)

    def some(step, _):
        local = []
        for u in range(TOGETHER):
            k = step * TOGETHER + u
            s, c = list_ref[k] // chunks, list_ref[k] % chunks
            doc = jnp.where(k < found, meta_ref[s], -1).astype(F32)
            rows = pl.ds(pl.multiple_of(c * ROWS, ROWS), ROWS)
            tokens = pl.ds(pl.multiple_of(s * BLOCK, BLOCK), BLOCK)
            scores = lax.dot_general(
                key_ref[tokens, :],
                q_ref[rows, :],
                (((1,), (1,)), ((), ())),
                preferred_element_type=F32,
            )
            alive = iota((BLOCK, ROWS), 0) < meta_ref[3 * slots + s]
            scores = jnp.where(alive, scores * scale, NEG)
            top = jnp.max(scores, axis=0, keepdims=True)
            probs = jnp.exp(scores - top)
            total = jnp.sum(probs, axis=0, keepdims=True)
            mixed = dot(value_ref[:, tokens], probs.astype(BF16))
            local.append((c, doc, top, total, mixed))
        for c, doc, top, total, mixed in local:
            one = pl.ds(c, 1)
            match = d_ref[one, :] == doc
            old = m_ref[one, :]
            new = jnp.where(match, jnp.maximum(old, top), old)
            left = jnp.exp(old - new)
            right = jnp.where(match, jnp.exp(top - new), 0.0)
            m_ref[one, :] = new
            l_ref[one, :] = l_ref[one, :] * left + total * right
            acc_ref[c] = acc_ref[c] * left + mixed * right
        return 0

    lax.fori_loop(0, (found + TOGETHER - 1) // TOGETHER, some, 0)

    facts = jnp.concatenate([m_ref[...], l_ref[...]], axis=0)
    pad = jnp.zeros((HD - 2 * chunks * PIECES, ROWS), F32)
    facts = jnp.transpose(jnp.concatenate(split(facts) + [pad], axis=0)).astype(BF16)
    turned = [jnp.transpose(acc_ref[c]) for c in range(chunks)]
    lane = iota((count, HD), 1)
    mine = (lane % CHUNK == iota((count, HD), 0) // CHUNK) & (lane < 2 * chunks * PIECES)
    lane, column = iota((HD, HD), 0), iota((HD, HD), 1)
    blocks = []
    packed = jnp.zeros((count, HD), F32)
    for h in range(QPG):
        at = slice(h * CHUNK, (h + 1) * CHUNK)
        blocks.append(jnp.concatenate([block[at] for block in turned], axis=0))
        fact = jnp.concatenate([facts[at]] * chunks, axis=0)
        fact = jnp.where(mine, fact, jnp.zeros_like(fact))
        pick = jnp.where(lane // chunks * QPG + h == column, 1.0, 0.0).astype(BF16)
        packed = packed + dot(fact, pick)
    blocks.append(packed)
    for h, block in enumerate(blocks):
        block = dot(unsort, block.astype(BF16)).astype(BF16)
        for k in range(quarters):
            out_refs[-k % quarters][h, :, :] = block[k * here : (k + 1) * here, :]


def merge_kernel(place_ref, query_ref, *refs):
    parts_refs, out_ref = refs[:-1], refs[-1]
    sources = len(parts_refs)
    _, here, _ = query_ref.shape
    owners = here // 8
    wide = QPG * HD
    lanes, head = iota((HD, wide), 0), iota((HD, wide), 1) // HD
    known = lanes < 2 * QPG * PIECES
    pick_m = jnp.where((lanes % (2 * QPG) == head) & known, 1.0, 0.0).astype(BF16)
    pick_l = jnp.where((lanes % (2 * QPG) == head + QPG) & known, 1.0, 0.0).astype(BF16)
    facts = [ref[QPG, :, :] for ref in parts_refs]
    tops = [dot(fact, pick_m) for fact in facts]
    totals = [dot(fact, pick_l) for fact in facts]
    top = tops[0]
    for s in range(1, sources):
        top = jnp.maximum(top, tops[s])
    total = jnp.zeros((here, wide), F32)
    mixed = [jnp.zeros((here, HD), F32)] * QPG
    for s in range(sources):
        weight = jnp.exp(tops[s] - top)
        total = total + weight * totals[s]
        for h in range(QPG):
            part = parts_refs[s][h, :, :].astype(F32)
            mixed[h] = mixed[h] + weight[:, h * HD : (h + 1) * HD] * part
    lane = iota((here, HD), 1)
    z = place_ref[0]
    base = (z + QPG // 2) % QPG * 16
    for h in range(QPG):
        query = query_ref[h, :, :].astype(F32)
        fact = jnp.where(lane // 16 == z, query, 0.0)
        pieces = split(top[:, h * HD : (h + 1) * HD]) + split(total[:, h * HD : (h + 1) * HD])
        for k, piece in enumerate(pieces):
            fact = jnp.where(lane == base + k, piece, fact)
        for i in range(owners):
            rows = slice(8 * i, 8 * i + 8)
            tile = jnp.concatenate([mixed[h][rows], fact[rows]], axis=0)
            out_ref[i * QPG + h, :, :] = tile.astype(BF16)


def finish_kernel(place_ref, parts_ref, key_ref, value_ref, out_ref):
    owners = parts_ref.shape[0] // QPG
    rows = key_ref.shape[0]
    x = place_ref[1]
    pick = jnp.where(iota((8, rows), 1) == iota((8, rows), 0) + 8 * x, 1.0, 0.0).astype(BF16)
    own_key, own_value = dot(pick, key_ref[...]), dot(pick, value_ref[...])
    lanes, column = iota((HD, 2 * HD), 0), iota((HD, 2 * HD), 1)
    lane = iota((8, HD), 1)
    spread = []
    for z in range(QPG):
        base = (z + QPG // 2) % QPG * 16
        low = jnp.where(column < HD, base, base + PIECES)
        pick = jnp.where((lanes >= low) & (lanes < low + PIECES), 1.0, 0.0).astype(BF16)
        fact = jnp.concatenate(
            [parts_ref[i * QPG + z, :, :].astype(F32)[8:] for i in range(owners)], axis=0
        )
        spread.append((dot(fact.astype(BF16), pick), fact))
    outs = []
    for i in range(owners):
        at, wide = slice(8 * i, 8 * i + 8), slice(i * HD, (i + 1) * HD)
        query = jnp.zeros((8, HD), F32)
        for z in range(QPG):
            query = jnp.where(lane // 16 == z, spread[z][1][at], query)
        own = jnp.sum(query * own_key[:, wide], axis=1, keepdims=True) * (HD ** (-0.5))
        own = jnp.broadcast_to(own, (8, HD))
        top = own
        for z in range(QPG):
            top = jnp.maximum(top, spread[z][0][at, :HD])
        total = jnp.exp(own - top)
        mixed = total * own_value[:, wide]
        for z in range(QPG):
            weight = jnp.exp(spread[z][0][at, :HD] - top)
            total = total + weight * spread[z][0][at, HD:]
            mixed = mixed + weight * parts_ref[i * QPG + z, :, :].astype(F32)[:8]
        outs.append(mixed / total)
    done = jnp.concatenate(outs, axis=0).astype(BF16)
    for k in range(out_ref.shape[0]):
        out_ref[k, :, :] = done


def place_kernel(place_ref, *refs):
    blocks, out_ref, held_ref = refs[:-2], refs[-2], refs[-1]
    quarters = len(blocks)
    depths, here, _ = blocks[0].shape
    x = place_ref[1]
    for k, ref in enumerate(blocks):
        held_ref[(x + quarters - k) % quarters] = ref[...]
    for x in range(0, quarters, 2):
        for z in range(depths):
            first = held_ref[x, z, :, :].astype(F32)
            second = held_ref[x + 1, z, :, :].astype(F32)
            for i in range(here // 8):
                rows = slice(8 * i, 8 * i + 8)
                at = (i * depths + z) * HD
                out_ref[8 * x : 8 * x + 16, at : at + HD] = jnp.concatenate(
                    [first[rows], second[rows]], axis=0
                ).astype(BF16)


def attend_call(meta, doc_col, doc_row, queries, keys, values):
    quarters = len(queries)
    count, here = doc_col.shape[0], queries[0].shape[1]
    slots = keys.shape[0] // BLOCK
    return pl.pallas_call(
        attend_kernel,
        out_shape=[jax.ShapeDtypeStruct((QPG + 1, here, HD), BF16)] * quarters,
        in_specs=[smem()] + [vmem()] * (4 + quarters),
        out_specs=[vmem()] * quarters,
        scratch_shapes=[
            pltpu.SMEM((slots * (count // CHUNK) + TOGETHER,), jnp.int32),
            pltpu.VMEM((count * QPG, HD), BF16),
            pltpu.VMEM((count // CHUNK, ROWS), F32),
            pltpu.VMEM((count // CHUNK, ROWS), F32),
            pltpu.VMEM((count // CHUNK, ROWS), F32),
            pltpu.VMEM((count // CHUNK, HD, ROWS), F32),
        ],
        compiler_params=pltpu.CompilerParams(vmem_limit_bytes=VMEM_BYTES),
    )(meta, doc_col, doc_row, *queries, keys, values)


def shift(block, axis, step):
    size = lax.axis_size(axis)
    return lax.ppermute(block, axis, [(i, (i + step) % size) for i in range(size)])


def per_device(
    hidden,
    q_weight,
    new_key,
    new_value,
    key_cache,
    value_cache,
    req_doc,
    doc_len,
    slot_doc,
    slot_blk,
):
    depths, quarters = lax.axis_size("z"), lax.axis_size("x")
    owners = lax.axis_size("y") * lax.axis_size("c")
    rows = hidden.shape[0]
    count = owners * rows
    here = count // quarters
    slots = slot_doc.shape[0]
    z, x = lax.axis_index("z"), lax.axis_index("x")
    place = jnp.stack([z, x])

    docs = req_doc.reshape(owners, quarters, rows // quarters).transpose(1, 0, 2)
    docs = docs[(x - jnp.arange(quarters)) % quarters].reshape(count)
    lower = jnp.sum((docs[None, :] < slot_doc[:, None]).astype(jnp.int32), axis=1)
    upper = jnp.sum((docs[None, :] <= slot_doc[:, None]).astype(jnp.int32), axis=1)
    doc_ids = jnp.arange(DOCS)
    slot_len = jnp.sum(
        jnp.where(slot_doc[:, None] == doc_ids[None, :], doc_len[None, :], 0), axis=1
    )
    remain = jnp.clip(slot_len - slot_blk * BLOCK, 0, BLOCK)
    first = lower // CHUNK
    last = jnp.where((upper > lower) & (remain > 0), (upper + CHUNK - 1) // CHUNK, first)
    meta = jnp.concatenate([slot_doc, first, last, remain])
    doc_col = jnp.broadcast_to(docs[:, None], (count, HD))
    doc_row = jnp.broadcast_to(docs[None, :], (8, count))

    order = (x + jnp.arange(quarters)) % quarters
    hidden = hidden.reshape(quarters, 8, -1)[order].reshape(rows, -1)
    partial = dot(hidden, q_weight).astype(jnp.float16)
    partial = [partial[8 * k : 8 * k + 8] for k in range(quarters)]
    partial = [partial[0]] + [shift(partial[k], "x", k) for k in range(1, quarters)]
    partial = sum(block.astype(F32) for block in partial).astype(jnp.float16)
    partial = partial.reshape(8, owners * QPG, HD).transpose(1, 0, 2)
    partial = lax.all_to_all(partial, ("y", "c", "z"), 0, 0, tiled=True)
    query = jnp.sum(partial.reshape(owners, depths, 8, HD).astype(F32), axis=1).astype(BF16)
    query = jnp.broadcast_to(query.reshape(1, here, HD), (depths, here, HD))
    query = lax.all_to_all(query, "z", 0, 0, tiled=True)
    queries = [query] + [shift(query, "x", k) for k in range(1, quarters)]
    parts = attend_call(meta, doc_col, doc_row, queries, key_cache[0], value_cache[0].T)
    parts = [parts[0]] + [shift(parts[k], "x", k) for k in range(1, quarters)]
    params = pltpu.CompilerParams(vmem_limit_bytes=VMEM_BYTES)
    parts = pl.pallas_call(
        merge_kernel,
        out_shape=jax.ShapeDtypeStruct((owners * QPG, 16, HD), BF16),
        in_specs=[smem()] + [vmem()] * (quarters + 1),
        out_specs=vmem(),
        compiler_params=params,
    )(place, query, *parts)
    parts = lax.all_to_all(parts, ("y", "c", "z"), 0, 0, tiled=True)
    result = pl.pallas_call(
        finish_kernel,
        out_shape=jax.ShapeDtypeStruct((depths, here, HD), BF16),
        in_specs=[smem(), vmem(), vmem(), vmem()],
        out_specs=vmem(),
        compiler_params=params,
    )(place, parts, new_key, new_value)
    result = lax.all_to_all(result, "z", 0, 0, tiled=True)
    result = [result] + [shift(result, "x", k) for k in range(1, quarters)]
    return pl.pallas_call(
        place_kernel,
        out_shape=jax.ShapeDtypeStruct((rows, owners * QPG * HD), BF16),
        in_specs=[smem()] + [vmem()] * quarters,
        out_specs=vmem(),
        scratch_shapes=[pltpu.VMEM((quarters, depths, here, HD), BF16)],
        compiler_params=params,
    )(place, *result)


def solution(mesh):
    sizes = (8, 4, 4, 2)
    mesh = Mesh(mesh.devices.reshape(sizes), ("z", "x", "y", "c"))
    kv, req = ("z", "x"), ("y", "c")
    return jax.shard_map(
        per_device,
        mesh=mesh,
        in_specs=(
            P(req, kv),
            P(kv, None),
            P(req, None),
            P(req, None),
            P(req, kv, None),
            P(req, kv, None),
            P(),
            P(),
            P(kv),
            P(kv),
        ),
        out_specs=P(req, None),
        check_vma=False,
    )
```

```python
import functools

import jax
import jax.numpy as jnp
from jax import lax
from jax.experimental import pallas as pl
from jax.experimental.pallas import tpu as pltpu
from jax.sharding import Mesh
from jax.sharding import PartitionSpec as P

HD = 128
QPG = 8
BLOCK = 512
DOCS = 24
CHUNK = 16
ROWS = CHUNK * QPG
TOGETHER = 4
PIECES = 3

NEG = -1e30
F32 = jnp.float32
BF16 = jnp.bfloat16
VMEM_BYTES = 16 * 1024 * 1024


def dot(a, b):
    return jnp.dot(a, b, preferred_element_type=F32)


def iota(shape, axis):
    return lax.broadcasted_iota(jnp.int32, shape, axis)


def vmem():
    return pl.BlockSpec(memory_space=pltpu.VMEM)


def smem():
    return pl.BlockSpec(memory_space=pltpu.SMEM)


def split(value):
    pieces = []
    for _ in range(PIECES):
        piece = value.astype(BF16).astype(F32)
        pieces.append(piece)
        value = value - piece
    return pieces


def plan_kernel(
    meta_ref, doc_col_ref, doc_row_ref, list_ref, sort_ref, unsort_ref, match_ref, *, slots
):
    count = doc_col_ref.shape[0]
    chunks = count // CHUNK
    found = 0
    for s in range(slots):

        def put(c, n, s=s):
            list_ref[n] = s * chunks + c
            return n + 1

        found = lax.fori_loop(meta_ref[slots + s], meta_ref[2 * slots + s], put, found)
    for u in range(TOGETHER):
        list_ref[found + u] = 0
    list_ref[slots * chunks + TOGETHER] = found

    col = doc_col_ref[:, :1]
    row = doc_row_ref[:1, :]
    down, across = iota((count, count), 0), iota((count, count), 1)
    before = jnp.where((col < row) | ((col == row) & (down < across)), 1.0, 0.0)
    rank_row = jnp.sum(before, axis=0, keepdims=True).astype(jnp.int32)
    behind = jnp.where((row < col) | ((row == col) & (across < down)), 1.0, 0.0)
    rank_col = jnp.sum(behind, axis=1, keepdims=True).astype(jnp.int32)
    unsort = jnp.where(across == rank_col, 1.0, 0.0).astype(BF16)
    sort_ref[...] = jnp.where(down == rank_row, 1.0, 0.0).astype(BF16)
    unsort_ref[...] = unsort
    docs = dot(doc_row_ref[...].astype(F32).astype(BF16), unsort)
    docs = jnp.concatenate([docs] * (chunks // 8), axis=0)
    docs = jnp.where(iota((chunks, count), 1) // CHUNK == iota((chunks, count), 0), docs, 0.0)
    same = iota((count, ROWS), 0) % CHUNK == iota((count, ROWS), 1) % CHUNK
    match_ref[...] = dot(docs.astype(BF16), jnp.where(same, 1.0, 0.0).astype(BF16))


def attend_kernel(meta_ref, list_ref, sort_ref, unsort_ref, d_ref, *refs):
    quarters = (len(refs) - 6) // 2
    query_refs, (key_ref, value_ref) = refs[:quarters], refs[quarters : quarters + 2]
    out_refs = refs[quarters + 2 : 2 * quarters + 2]
    q_ref, m_ref, l_ref, acc_ref = refs[2 * quarters + 2 :]
    count = sort_ref.shape[0]
    chunks = count // CHUNK
    slots = key_ref.shape[0] // BLOCK
    here = count // quarters
    scale = HD ** (-0.5)
    found = list_ref[slots * chunks + TOGETHER]
    sort, unsort = sort_ref[...], unsort_ref[...]
    for h in range(QPG):
        blocks = jnp.concatenate([ref[h, :, :] for ref in query_refs], axis=0)
        ordered = dot(sort, blocks).astype(BF16)
        for c in range(chunks):
            at = c * ROWS + h * CHUNK
            q_ref[at : at + CHUNK, :] = ordered[c * CHUNK : (c + 1) * CHUNK, :]
    m_ref[...] = jnp.full_like(m_ref, NEG)
    l_ref[...] = jnp.zeros_like(l_ref)
    acc_ref[...] = jnp.zeros_like(acc_ref)

    def some(step, _):
        local = []
        for u in range(TOGETHER):
            k = step * TOGETHER + u
            s, c = list_ref[k] // chunks, list_ref[k] % chunks
            doc = jnp.where(k < found, meta_ref[s], -1).astype(F32)
            rows = pl.ds(pl.multiple_of(c * ROWS, ROWS), ROWS)
            tokens = pl.ds(pl.multiple_of(s * BLOCK, BLOCK), BLOCK)
            scores = lax.dot_general(
                key_ref[tokens, :],
                q_ref[rows, :],
                (((1,), (1,)), ((), ())),
                preferred_element_type=F32,
            )
            alive = iota((BLOCK, ROWS), 0) < meta_ref[3 * slots + s]
            scores = jnp.where(alive, scores * scale, NEG)
            top = jnp.max(scores, axis=0, keepdims=True)
            probs = jnp.exp(scores - top)
            total = jnp.sum(probs, axis=0, keepdims=True)
            mixed = dot(value_ref[:, tokens], probs.astype(BF16))
            local.append((c, doc, top, total, mixed))
        for c, doc, top, total, mixed in local:
            one = pl.ds(c, 1)
            match = d_ref[one, :] == doc
            old = m_ref[one, :]
            new = jnp.where(match, jnp.maximum(old, top), old)
            left = jnp.exp(old - new)
            right = jnp.where(match, jnp.exp(top - new), 0.0)
            m_ref[one, :] = new
            l_ref[one, :] = l_ref[one, :] * left + total * right
            acc_ref[c] = acc_ref[c] * left + mixed * right
        return 0

    lax.fori_loop(0, (found + TOGETHER - 1) // TOGETHER, some, 0)

    facts = jnp.concatenate([m_ref[...], l_ref[...]], axis=0)
    pad = jnp.zeros((HD - 2 * chunks * PIECES, ROWS), F32)
    facts = jnp.transpose(jnp.concatenate(split(facts) + [pad], axis=0)).astype(BF16)
    turned = [jnp.transpose(acc_ref[c]) for c in range(chunks)]
    lane = iota((count, HD), 1)
    mine = (lane % CHUNK == iota((count, HD), 0) // CHUNK) & (lane < 2 * chunks * PIECES)
    lane, column = iota((HD, HD), 0), iota((HD, HD), 1)
    blocks = []
    packed = jnp.zeros((count, HD), F32)
    for h in range(QPG):
        at = slice(h * CHUNK, (h + 1) * CHUNK)
        blocks.append(jnp.concatenate([block[at] for block in turned], axis=0))
        fact = jnp.concatenate([facts[at]] * chunks, axis=0)
        fact = jnp.where(mine, fact, jnp.zeros_like(fact))
        pick = jnp.where(lane // chunks * QPG + h == column, 1.0, 0.0).astype(BF16)
        packed = packed + dot(fact, pick)
    blocks.append(packed)
    for h, block in enumerate(blocks):
        block = dot(unsort, block.astype(BF16)).astype(BF16)
        for k in range(quarters):
            out_refs[-k % quarters][h, :, :] = block[k * here : (k + 1) * here, :]


def spread_kernel(parts_ref, out_ref):
    copies, here, _ = out_ref.shape
    total = parts_ref[:, 0, :, :]
    for z in range(1, parts_ref.shape[1]):
        total = total + parts_ref[:, z, :, :]
    query = total.reshape(here, HD).astype(BF16)
    for k in range(copies):
        out_ref[k, :, :] = query


def merge_kernel(place_ref, query_ref, *refs):
    parts_refs, out_ref = refs[:-1], refs[-1]
    sources = len(parts_refs)
    _, here, _ = query_ref.shape
    owners = here // 8
    wide = QPG * HD
    lanes, head = iota((HD, wide), 0), iota((HD, wide), 1) // HD
    known = lanes < 2 * QPG * PIECES
    pick_m = jnp.where((lanes % (2 * QPG) == head) & known, 1.0, 0.0).astype(BF16)
    pick_l = jnp.where((lanes % (2 * QPG) == head + QPG) & known, 1.0, 0.0).astype(BF16)
    facts = [ref[QPG, :, :] for ref in parts_refs]
    tops = [dot(fact, pick_m) for fact in facts]
    totals = [dot(fact, pick_l) for fact in facts]
    top = tops[0]
    for s in range(1, sources):
        top = jnp.maximum(top, tops[s])
    total = jnp.zeros((here, wide), F32)
    mixed = [jnp.zeros((here, HD), F32)] * QPG
    for s in range(sources):
        weight = jnp.exp(tops[s] - top)
        total = total + weight * totals[s]
        for h in range(QPG):
            part = parts_refs[s][h, :, :].astype(F32)
            mixed[h] = mixed[h] + weight[:, h * HD : (h + 1) * HD] * part
    lane = iota((here, HD), 1)
    z = place_ref[0]
    base = (z + QPG // 2) % QPG * 16
    for h in range(QPG):
        query = query_ref[h, :, :].astype(F32)
        fact = jnp.where(lane // 16 == z, query, 0.0)
        pieces = split(top[:, h * HD : (h + 1) * HD]) + split(total[:, h * HD : (h + 1) * HD])
        for k, piece in enumerate(pieces):
            fact = jnp.where(lane == base + k, piece, fact)
        for i in range(owners):
            rows = slice(8 * i, 8 * i + 8)
            tile = jnp.concatenate([mixed[h][rows], fact[rows]], axis=0)
            out_ref[i * QPG + h, :, :] = tile.astype(BF16)


def finish_kernel(place_ref, parts_ref, key_ref, value_ref, out_ref):
    owners = parts_ref.shape[0] // QPG
    rows = key_ref.shape[0]
    x = place_ref[1]
    pick = jnp.where(iota((8, rows), 1) == iota((8, rows), 0) + 8 * x, 1.0, 0.0).astype(BF16)
    own_key, own_value = dot(pick, key_ref[...]), dot(pick, value_ref[...])
    lanes, column = iota((HD, 2 * HD), 0), iota((HD, 2 * HD), 1)
    lane = iota((8, HD), 1)
    spread = []
    for z in range(QPG):
        base = (z + QPG // 2) % QPG * 16
        low = jnp.where(column < HD, base, base + PIECES)
        pick = jnp.where((lanes >= low) & (lanes < low + PIECES), 1.0, 0.0).astype(BF16)
        fact = jnp.concatenate(
            [parts_ref[i * QPG + z, :, :].astype(F32)[8:] for i in range(owners)], axis=0
        )
        spread.append((dot(fact.astype(BF16), pick), fact))
    outs = []
    for i in range(owners):
        at, wide = slice(8 * i, 8 * i + 8), slice(i * HD, (i + 1) * HD)
        query = jnp.zeros((8, HD), F32)
        for z in range(QPG):
            query = jnp.where(lane // 16 == z, spread[z][1][at], query)
        own = jnp.sum(query * own_key[:, wide], axis=1, keepdims=True) * (HD ** (-0.5))
        own = jnp.broadcast_to(own, (8, HD))
        top = own
        for z in range(QPG):
            top = jnp.maximum(top, spread[z][0][at, :HD])
        total = jnp.exp(own - top)
        mixed = total * own_value[:, wide]
        for z in range(QPG):
            weight = jnp.exp(spread[z][0][at, :HD] - top)
            total = total + weight * spread[z][0][at, HD:]
            mixed = mixed + weight * parts_ref[i * QPG + z, :, :].astype(F32)[:8]
        outs.append(mixed / total)
    done = jnp.concatenate(outs, axis=0).astype(BF16)
    for k in range(out_ref.shape[0]):
        out_ref[k, :, :] = done


def place_kernel(place_ref, *refs):
    blocks, out_ref, held_ref = refs[:-2], refs[-2], refs[-1]
    quarters = len(blocks)
    depths, here, _ = blocks[0].shape
    x = place_ref[1]
    for k, ref in enumerate(blocks):
        held_ref[(x + quarters - k) % quarters] = ref[...]
    for x in range(0, quarters, 2):
        for z in range(depths):
            first = held_ref[x, z, :, :].astype(F32)
            second = held_ref[x + 1, z, :, :].astype(F32)
            for i in range(here // 8):
                rows = slice(8 * i, 8 * i + 8)
                at = (i * depths + z) * HD
                out_ref[8 * x : 8 * x + 16, at : at + HD] = jnp.concatenate(
                    [first[rows], second[rows]], axis=0
                ).astype(BF16)


def plan_call(meta, doc_col, doc_row, slots):
    count = doc_col.shape[0]
    chunks = count // CHUNK
    return pl.pallas_call(
        functools.partial(plan_kernel, slots=slots),
        out_shape=[
            jax.ShapeDtypeStruct((slots * chunks + TOGETHER + 1,), jnp.int32),
            jax.ShapeDtypeStruct((count, count), BF16),
            jax.ShapeDtypeStruct((count, count), BF16),
            jax.ShapeDtypeStruct((chunks, ROWS), F32),
        ],
        in_specs=[smem(), vmem(), vmem()],
        out_specs=[smem(), vmem(), vmem(), vmem()],
        compiler_params=pltpu.CompilerParams(vmem_limit_bytes=VMEM_BYTES),
        cost_estimate=pl.CostEstimate(
            flops=2 * count**3, bytes_accessed=8 * count * count, transcendentals=0
        ),
    )(meta, doc_col, doc_row)


def attend_call(meta, plan, queries, keys, values):
    quarters = len(queries)
    here = queries[0].shape[1]
    count = quarters * here
    return pl.pallas_call(
        attend_kernel,
        out_shape=[jax.ShapeDtypeStruct((QPG + 1, here, HD), BF16)] * quarters,
        in_specs=[smem(), smem()] + [vmem()] * (5 + quarters),
        out_specs=[vmem()] * quarters,
        scratch_shapes=[
            pltpu.VMEM((count * QPG, HD), BF16),
            pltpu.VMEM((count // CHUNK, ROWS), F32),
            pltpu.VMEM((count // CHUNK, ROWS), F32),
            pltpu.VMEM((count // CHUNK, HD, ROWS), F32),
        ],
        compiler_params=pltpu.CompilerParams(vmem_limit_bytes=VMEM_BYTES),
    )(meta, *plan, *queries, keys, values)


def shift(block, axis, step):
    size = lax.axis_size(axis)
    return lax.ppermute(block, axis, [(i, (i + step) % size) for i in range(size)])


def per_device(
    hidden,
    q_weight,
    new_key,
    new_value,
    key_cache,
    value_cache,
    req_doc,
    doc_len,
    slot_doc,
    slot_blk,
):
    depths, quarters = lax.axis_size("z"), lax.axis_size("x")
    owners = lax.axis_size("y") * lax.axis_size("c")
    rows = hidden.shape[0]
    count = owners * rows
    here = count // quarters
    slots = slot_doc.shape[0]
    z, x = lax.axis_index("z"), lax.axis_index("x")
    place = jnp.stack([z, x])

    docs = req_doc.reshape(owners, quarters, rows // quarters).transpose(1, 0, 2)
    docs = docs[(x - jnp.arange(quarters)) % quarters].reshape(count)
    lower = jnp.sum((docs[None, :] < slot_doc[:, None]).astype(jnp.int32), axis=1)
    upper = jnp.sum((docs[None, :] <= slot_doc[:, None]).astype(jnp.int32), axis=1)
    doc_ids = jnp.arange(DOCS)
    slot_len = jnp.sum(
        jnp.where(slot_doc[:, None] == doc_ids[None, :], doc_len[None, :], 0), axis=1
    )
    remain = jnp.clip(slot_len - slot_blk * BLOCK, 0, BLOCK)
    first = lower // CHUNK
    last = jnp.where((upper > lower) & (remain > 0), (upper + CHUNK - 1) // CHUNK, first)
    meta = jnp.concatenate([slot_doc, first, last, remain])
    doc_col = jnp.broadcast_to(docs[:, None], (count, HD))
    doc_row = jnp.broadcast_to(docs[None, :], (8, count))

    params = pltpu.CompilerParams(vmem_limit_bytes=VMEM_BYTES)
    plan = plan_call(meta, doc_col, doc_row, slots)
    partial = dot(hidden, q_weight).astype(jnp.float16)
    partial = [
        lax.dynamic_slice_in_dim(partial, (x + k) % quarters * 8, 8, 0) for k in range(quarters)
    ]
    partial = [partial[0]] + [shift(partial[k], "x", k) for k in range(1, quarters)]
    partial = sum(block.astype(F32) for block in partial).astype(jnp.float16)
    partial, meta, plan = lax.optimization_barrier((partial, meta, plan))
    partial = partial.reshape(8, owners * QPG, HD).transpose(1, 0, 2)
    partial = lax.all_to_all(partial, ("y", "c", "z"), 0, 0, tiled=True)
    query = pl.pallas_call(
        spread_kernel,
        out_shape=jax.ShapeDtypeStruct((depths, here, HD), BF16),
        in_specs=[vmem()],
        out_specs=vmem(),
        compiler_params=params,
    )(partial.reshape(owners, depths, 8, HD).astype(F32))
    query = lax.all_to_all(query, "z", 0, 0, tiled=True)
    queries = [query] + [shift(query, "x", k) for k in range(1, quarters)]
    parts = attend_call(meta, plan, queries, key_cache[0], value_cache[0].T)
    parts = [parts[0]] + [shift(parts[k], "x", k) for k in range(1, quarters)]
    parts = pl.pallas_call(
        merge_kernel,
        out_shape=jax.ShapeDtypeStruct((owners * QPG, 16, HD), BF16),
        in_specs=[smem()] + [vmem()] * (quarters + 1),
        out_specs=vmem(),
        compiler_params=params,
    )(place, query, *parts)
    parts = lax.all_to_all(parts, ("y", "c", "z"), 0, 0, tiled=True)
    result = pl.pallas_call(
        finish_kernel,
        out_shape=jax.ShapeDtypeStruct((depths, here, HD), BF16),
        in_specs=[smem(), vmem(), vmem(), vmem()],
        out_specs=vmem(),
        compiler_params=params,
    )(place, parts, new_key, new_value)
    result = lax.all_to_all(result, "z", 0, 0, tiled=True)
    result = [result] + [shift(result, "x", k) for k in range(1, quarters)]
    return pl.pallas_call(
        place_kernel,
        out_shape=jax.ShapeDtypeStruct((rows, owners * QPG * HD), BF16),
        in_specs=[smem()] + [vmem()] * quarters,
        out_specs=vmem(),
        scratch_shapes=[pltpu.VMEM((quarters, depths, here, HD), BF16)],
        compiler_params=params,
    )(place, *result)


def solution(mesh):
    sizes = (8, 4, 4, 2)
    mesh = Mesh(mesh.devices.reshape(sizes), ("z", "x", "y", "c"))
    kv, req = ("z", "x"), ("y", "c")
    return jax.shard_map(
        per_device,
        mesh=mesh,
        in_specs=(
            P(req, kv),
            P(kv, None),
            P(req, None),
            P(req, None),
            P(req, kv, None),
            P(req, kv, None),
            P(),
            P(),
            P(kv),
            P(kv),
        ),
        out_specs=P(req, None),
        check_vma=False,
    )
```

```python
import functools

import jax
import jax.numpy as jnp
from jax import lax
from jax.experimental import pallas as pl
from jax.experimental.pallas import tpu as pltpu
from jax.sharding import Mesh
from jax.sharding import PartitionSpec as P

HD = 128
QPG = 8
BLOCK = 512
DOCS = 24
CHUNK = 16
ROWS = CHUNK * QPG
TOGETHER = 8
PIECES = 3
HALF = HD // 2

NEG = -1e30
F32 = jnp.float32
BF16 = jnp.bfloat16
VMEM_BYTES = 16 * 1024 * 1024


def dot(a, b):
    return jnp.dot(a, b, preferred_element_type=F32)


def iota(shape, axis):
    return lax.broadcasted_iota(jnp.int32, shape, axis)


def vmem():
    return pl.BlockSpec(memory_space=pltpu.VMEM)


def smem():
    return pl.BlockSpec(memory_space=pltpu.SMEM)


def split(value):
    pieces = []
    for _ in range(PIECES):
        piece = value.astype(BF16).astype(F32)
        pieces.append(piece)
        value = value - piece
    return pieces


def plan_kernel(
    meta_ref, doc_col_ref, doc_row_ref, list_ref, sort_ref, unsort_ref, match_ref, *, slots
):
    count = doc_col_ref.shape[0]
    chunks = count // CHUNK
    found = 0
    for s in range(slots):

        def put(c, n, s=s):
            list_ref[n] = s * chunks + c
            return n + 1

        found = lax.fori_loop(meta_ref[slots + s], meta_ref[2 * slots + s], put, found)
    for u in range(TOGETHER):
        list_ref[found + u] = 0
    list_ref[slots * chunks + TOGETHER] = found

    col = doc_col_ref[:, :1]
    row = doc_row_ref[:1, :]
    down, across = iota((count, count), 0), iota((count, count), 1)
    before = jnp.where((col < row) | ((col == row) & (down < across)), 1.0, 0.0)
    rank_row = jnp.sum(before, axis=0, keepdims=True).astype(jnp.int32)
    behind = jnp.where((row < col) | ((row == col) & (across < down)), 1.0, 0.0)
    rank_col = jnp.sum(behind, axis=1, keepdims=True).astype(jnp.int32)
    unsort = jnp.where(across == rank_col, 1.0, 0.0).astype(BF16)
    sort_ref[...] = jnp.where(down == rank_row, 1.0, 0.0).astype(BF16)
    unsort_ref[...] = unsort
    docs = dot(doc_row_ref[...].astype(F32).astype(BF16), unsort)
    docs = jnp.concatenate([docs] * (chunks // 8), axis=0)
    docs = jnp.where(iota((chunks, count), 1) // CHUNK == iota((chunks, count), 0), docs, 0.0)
    same = iota((count, ROWS), 0) % CHUNK == iota((count, ROWS), 1) % CHUNK
    match_ref[...] = dot(docs.astype(BF16), jnp.where(same, 1.0, 0.0).astype(BF16))


def attend_kernel(meta_ref, list_ref, sort_ref, unsort_ref, d_ref, *refs):
    quarters = (len(refs) - 6) // 2
    query_refs, (key_ref, value_ref) = refs[:quarters], refs[quarters : quarters + 2]
    out_refs = refs[quarters + 2 : 2 * quarters + 2]
    q_ref, m_ref, l_ref, acc_ref = refs[2 * quarters + 2 :]
    count = sort_ref.shape[0]
    chunks = count // CHUNK
    slots = key_ref.shape[0] // BLOCK
    here = count // quarters
    scale = HD ** (-0.5)
    found = list_ref[slots * chunks + TOGETHER]
    sort, unsort = sort_ref[...], unsort_ref[...]
    for h in range(QPG):
        blocks = jnp.concatenate([ref[h, :, :] for ref in query_refs], axis=0)
        ordered = dot(sort, blocks).astype(BF16)
        for c in range(chunks):
            at = c * ROWS + h * CHUNK
            q_ref[at : at + CHUNK, :] = ordered[c * CHUNK : (c + 1) * CHUNK, :]
    m_ref[...] = jnp.full_like(m_ref, NEG)
    l_ref[...] = jnp.zeros_like(l_ref)
    acc_ref[...] = jnp.zeros_like(acc_ref)

    def some(step, _):
        local = []
        for u in range(TOGETHER):
            k = step * TOGETHER + u
            s, c = list_ref[k] // chunks, list_ref[k] % chunks
            doc = jnp.where(k < found, meta_ref[s], -1).astype(F32)
            rows = pl.ds(pl.multiple_of(c * ROWS, ROWS), ROWS)
            tokens = pl.ds(pl.multiple_of(s * BLOCK, BLOCK), BLOCK)
            scores = lax.dot_general(
                key_ref[tokens, :],
                q_ref[rows, :],
                (((1,), (1,)), ((), ())),
                preferred_element_type=F32,
            )
            alive = iota((BLOCK, ROWS), 0) < meta_ref[3 * slots + s]
            scores = jnp.where(alive, scores * scale, NEG)
            top = jnp.max(scores, axis=0, keepdims=True)
            probs = jnp.exp(scores - top)
            total = jnp.sum(probs, axis=0, keepdims=True)
            mixed = dot(value_ref[:, tokens], probs.astype(BF16))
            local.append((c, doc, top, total, mixed))
        for c, doc, top, total, mixed in local:
            one = pl.ds(c, 1)
            match = d_ref[one, :] == doc
            old = m_ref[one, :]
            new = jnp.where(match, jnp.maximum(old, top), old)
            left = jnp.exp(old - new)
            right = jnp.where(match, jnp.exp(top - new), 0.0)
            m_ref[one, :] = new
            l_ref[one, :] = l_ref[one, :] * left + total * right
            acc_ref[c] = acc_ref[c] * left + mixed * right
        return 0

    lax.fori_loop(0, (found + TOGETHER - 1) // TOGETHER, some, 0)

    facts = jnp.concatenate([m_ref[...], l_ref[...]], axis=0)
    pad = jnp.zeros((HD - 2 * chunks * PIECES, ROWS), F32)
    facts = jnp.transpose(jnp.concatenate(split(facts) + [pad], axis=0)).astype(BF16)
    turned = [jnp.transpose(acc_ref[c]) for c in range(chunks)]
    lane = iota((count, HD), 1)
    mine = (lane % CHUNK == iota((count, HD), 0) // CHUNK) & (lane < 2 * chunks * PIECES)
    lane, column = iota((HD, HD), 0), iota((HD, HD), 1)
    blocks = []
    packed = jnp.zeros((count, HD), F32)
    for h in range(QPG):
        at = slice(h * CHUNK, (h + 1) * CHUNK)
        blocks.append(jnp.concatenate([block[at] for block in turned], axis=0))
        fact = jnp.concatenate([facts[at]] * chunks, axis=0)
        fact = jnp.where(mine, fact, jnp.zeros_like(fact))
        pick = jnp.where(lane // chunks * QPG + h == column, 1.0, 0.0).astype(BF16)
        packed = packed + dot(fact, pick)
    blocks.append(packed)
    for h, block in enumerate(blocks):
        block = dot(unsort, block.astype(BF16)).astype(BF16)
        for k in range(quarters):
            out_refs[-k % quarters][h, :, :] = block[k * here : (k + 1) * here, :]


def spread_kernel(parts_ref, out_ref):
    copies, here, _ = out_ref.shape
    total = parts_ref[:, 0, :, :]
    for z in range(1, parts_ref.shape[1]):
        total = total + parts_ref[:, z, :, :]
    query = total.reshape(here, HD).astype(BF16)
    for k in range(copies):
        out_ref[k, :, :] = query


def merge_kernel(place_ref, query_ref, *refs):
    parts_refs, out_ref = refs[:-1], refs[-1]
    sources = len(parts_refs)
    _, here, _ = query_ref.shape
    wide = QPG * HD
    lanes, head = iota((HD, wide), 0), iota((HD, wide), 1) // HD
    known = lanes < 2 * QPG * PIECES
    pick_m = jnp.where((lanes % (2 * QPG) == head) & known, 1.0, 0.0).astype(BF16)
    pick_l = jnp.where((lanes % (2 * QPG) == head + QPG) & known, 1.0, 0.0).astype(BF16)
    facts = [ref[QPG, :, :] for ref in parts_refs]
    tops = [dot(fact, pick_m) for fact in facts]
    totals = [dot(fact, pick_l) for fact in facts]
    top = tops[0]
    for s in range(1, sources):
        top = jnp.maximum(top, tops[s])
    total = jnp.zeros((here, wide), F32)
    mixed = [jnp.zeros((here, HD), F32)] * QPG
    for s in range(sources):
        weight = jnp.exp(tops[s] - top)
        total = total + weight * totals[s]
        for h in range(QPG):
            part = parts_refs[s][h, :, :].astype(F32)
            mixed[h] = mixed[h] + weight[:, h * HD : (h + 1) * HD] * part
    lane = iota((here, HD), 1) % HALF
    z = place_ref[0]
    down, across = iota((HD, HD), 0), iota((HD, HD), 1) % HALF
    pick = jnp.where((across < 16) & (down == 16 * z + across), 1.0, 0.0).astype(BF16)
    left = iota((8, HD), 1) < HALF
    for h in range(QPG):
        fact = dot(query_ref[h, :, :], pick)
        pieces = split(top[:, h * HD : (h + 1) * HD]) + split(total[:, h * HD : (h + 1) * HD])
        for k, piece in enumerate(pieces):
            fact = jnp.where(lane == 16 + k, piece, fact)
        for y in range(here // 16):
            at = 16 * y
            facts = jnp.where(left, fact[at : at + 8], fact[at + 8 : at + 16])
            tile = jnp.concatenate([mixed[h][at : at + 16], facts], axis=0)
            out_ref[y * QPG + h, :, :] = tile.astype(BF16)


def finish_kernel(place_ref, parts_ref, key_ref, value_ref, other_ref, mine_ref, give_ref):
    depths, rows = QPG, key_ref.shape[0]
    lines = parts_ref.shape[0] // depths
    x, c = place_ref[1], place_ref[2]
    pick = jnp.where(iota((8, rows), 1) == iota((8, rows), 0) + 8 * x, 1.0, 0.0).astype(BF16)
    own = [dot(pick, ref[...]) for ref in (key_ref, value_ref)]
    other = [dot(pick, other_ref[k * rows : (k + 1) * rows, :]) for k in range(2)]
    lanes, column = iota((HD, 4 * HD), 0), iota((HD, 4 * HD), 1)
    low = column // (2 * HD) * HALF + 16 + column // HD % 2 * PIECES
    pick = jnp.where((lanes >= low) & (lanes < low + PIECES), 1.0, 0.0).astype(BF16)
    facts, spread = [], []
    for z in range(depths):
        fact = jnp.concatenate(
            [parts_ref[y * depths + z, :, :].astype(F32)[16:] for y in range(lines)], axis=0
        )
        facts.append(fact)
        spread.append(dot(fact.astype(BF16), pick))
    lane = iota((8 * lines, HD), 1) // 16
    mine, give = [], []
    queries = []
    for e in range(2):
        query = jnp.zeros((8 * lines, HD), F32)
        for z in range(depths):
            turned = pltpu.roll(facts[z], (16 * z - HALF * e) % HD, 1)
            query = jnp.where(lane == z, turned, query)
        queries.append(query)
    for y in range(lines):
        at = slice(8 * y, 8 * y + 8)
        done = []
        for e in range(2):
            key, value = [
                jnp.where(
                    c == 0,
                    block[:, 2 * y * HD : (2 * y + 1) * HD],
                    block[:, (2 * y + 1) * HD : (2 * y + 2) * HD],
                )
                for block in [jnp.where(c == e, a, b) for a, b in zip(own, other)]
            ]
            score = jnp.sum(queries[e][at] * key, axis=1, keepdims=True) * (HD ** (-0.5))
            score = jnp.broadcast_to(score, (8, HD))
            tops = [block[at, 2 * e * HD : (2 * e + 1) * HD] for block in spread]
            totals = [block[at, (2 * e + 1) * HD : (2 * e + 2) * HD] for block in spread]
            top = score
            for z in range(depths):
                top = jnp.maximum(top, tops[z])
            total = jnp.exp(score - top)
            mixed = total * value
            for z in range(depths):
                weight = jnp.exp(tops[z] - top)
                total = total + weight * totals[z]
                part = parts_ref[y * depths + z, :, :].astype(F32)[8 * e : 8 * e + 8]
                mixed = mixed + weight * part
            done.append(mixed / total)
        mine.append(jnp.where(c == 0, done[0], done[1]))
        give.append(jnp.where(c == 0, done[1], done[0]))
    mine_ref[...] = jnp.concatenate(mine, axis=0).astype(BF16)
    give_ref[...] = jnp.concatenate(give, axis=0).astype(BF16)


def join_kernel(place_ref, mine_ref, got_ref, out_ref):
    c = place_ref[2]
    mine, got = mine_ref[...].astype(F32), got_ref[...].astype(F32)
    first, second = jnp.where(c == 0, mine, got), jnp.where(c == 0, got, mine)
    rows = []
    for y in range(mine.shape[0] // 8):
        at = slice(8 * y, 8 * y + 8)
        rows += [first[at], second[at]]
    joined = jnp.concatenate(rows, axis=0).astype(BF16)
    for k in range(out_ref.shape[0]):
        out_ref[k, :, :] = joined


def place_kernel(place_ref, *refs):
    blocks, out_ref, held_ref = refs[:-2], refs[-2], refs[-1]
    quarters = len(blocks)
    depths, here, _ = blocks[0].shape
    x = place_ref[1]
    for k, ref in enumerate(blocks):
        held_ref[(x + quarters - k) % quarters] = ref[...]
    for x in range(0, quarters, 2):
        for z in range(depths):
            first = held_ref[x, z, :, :].astype(F32)
            second = held_ref[x + 1, z, :, :].astype(F32)
            for i in range(here // 8):
                rows = slice(8 * i, 8 * i + 8)
                at = (i * depths + z) * HD
                out_ref[8 * x : 8 * x + 16, at : at + HD] = jnp.concatenate(
                    [first[rows], second[rows]], axis=0
                ).astype(BF16)


def plan_call(meta, doc_col, doc_row, slots):
    count = doc_col.shape[0]
    chunks = count // CHUNK
    return pl.pallas_call(
        functools.partial(plan_kernel, slots=slots),
        out_shape=[
            jax.ShapeDtypeStruct((slots * chunks + TOGETHER + 1,), jnp.int32),
            jax.ShapeDtypeStruct((count, count), BF16),
            jax.ShapeDtypeStruct((count, count), BF16),
            jax.ShapeDtypeStruct((chunks, ROWS), F32),
        ],
        in_specs=[smem(), vmem(), vmem()],
        out_specs=[smem(), vmem(), vmem(), vmem()],
        compiler_params=pltpu.CompilerParams(vmem_limit_bytes=VMEM_BYTES),
        cost_estimate=pl.CostEstimate(
            flops=2 * count**3, bytes_accessed=8 * count * count, transcendentals=0
        ),
    )(meta, doc_col, doc_row)


def attend_call(meta, plan, queries, keys, values):
    quarters = len(queries)
    here = queries[0].shape[1]
    count = quarters * here
    return pl.pallas_call(
        attend_kernel,
        out_shape=[jax.ShapeDtypeStruct((QPG + 1, here, HD), BF16)] * quarters,
        in_specs=[smem(), smem()] + [vmem()] * (5 + quarters),
        out_specs=[vmem()] * quarters,
        scratch_shapes=[
            pltpu.VMEM((count * QPG, HD), BF16),
            pltpu.VMEM((count // CHUNK, ROWS), F32),
            pltpu.VMEM((count // CHUNK, ROWS), F32),
            pltpu.VMEM((count // CHUNK, HD, ROWS), F32),
        ],
        compiler_params=pltpu.CompilerParams(vmem_limit_bytes=VMEM_BYTES),
    )(meta, *plan, *queries, keys, values)


def shift(block, axis, step):
    size = lax.axis_size(axis)
    return lax.ppermute(block, axis, [(i, (i + step) % size) for i in range(size)])


def per_device(
    hidden,
    q_weight,
    new_key,
    new_value,
    key_cache,
    value_cache,
    req_doc,
    doc_len,
    slot_doc,
    slot_blk,
):
    depths, quarters = lax.axis_size("z"), lax.axis_size("x")
    owners = lax.axis_size("y") * lax.axis_size("c")
    rows = hidden.shape[0]
    count = owners * rows
    here = count // quarters
    slots = slot_doc.shape[0]
    z, x = lax.axis_index("z"), lax.axis_index("x")
    place = jnp.stack([z, x, lax.axis_index("c")])

    docs = req_doc.reshape(owners, quarters, rows // quarters).transpose(1, 0, 2)
    docs = docs[(x - jnp.arange(quarters)) % quarters].reshape(count)
    lower = jnp.sum((docs[None, :] < slot_doc[:, None]).astype(jnp.int32), axis=1)
    upper = jnp.sum((docs[None, :] <= slot_doc[:, None]).astype(jnp.int32), axis=1)
    doc_ids = jnp.arange(DOCS)
    slot_len = jnp.sum(
        jnp.where(slot_doc[:, None] == doc_ids[None, :], doc_len[None, :], 0), axis=1
    )
    remain = jnp.clip(slot_len - slot_blk * BLOCK, 0, BLOCK)
    first = lower // CHUNK
    last = jnp.where((upper > lower) & (remain > 0), (upper + CHUNK - 1) // CHUNK, first)
    meta = jnp.concatenate([slot_doc, first, last, remain])
    doc_col = jnp.broadcast_to(docs[:, None], (count, HD))
    doc_row = jnp.broadcast_to(docs[None, :], (8, count))

    params = pltpu.CompilerParams(vmem_limit_bytes=VMEM_BYTES)
    plan = plan_call(meta, doc_col, doc_row, slots)
    partial = dot(hidden, q_weight).astype(jnp.float16)
    partial = [
        lax.dynamic_slice_in_dim(partial, (x + k) % quarters * 8, 8, 0) for k in range(quarters)
    ]
    partial = [partial[0]] + [shift(partial[k], "x", k) for k in range(1, quarters)]
    partial = sum(block.astype(F32) for block in partial).astype(jnp.float16)
    partial, meta, plan = lax.optimization_barrier((partial, meta, plan))
    partial = partial.reshape(8, owners * QPG, HD).transpose(1, 0, 2)
    partial = lax.all_to_all(partial, ("y", "c", "z"), 0, 0, tiled=True)
    query = pl.pallas_call(
        spread_kernel,
        out_shape=jax.ShapeDtypeStruct((depths, here, HD), BF16),
        in_specs=[vmem()],
        out_specs=vmem(),
        compiler_params=params,
    )(partial.reshape(owners, depths, 8, HD).astype(F32))
    query = lax.all_to_all(query, "z", 0, 0, tiled=True)
    queries = [query] + [shift(query, "x", k) for k in range(1, quarters)]
    parts = attend_call(meta, plan, queries, key_cache[0], value_cache[0].T)
    parts = [parts[0]] + [shift(parts[k], "x", k) for k in range(1, quarters)]
    other = shift(jnp.concatenate([new_key, new_value], axis=0), "c", 1)
    parts, other = lax.optimization_barrier((parts, other))
    parts = pl.pallas_call(
        merge_kernel,
        out_shape=jax.ShapeDtypeStruct((owners // 2 * QPG, 24, HD), BF16),
        in_specs=[smem()] + [vmem()] * (quarters + 1),
        out_specs=vmem(),
        compiler_params=params,
    )(place, query, *parts)
    parts = lax.all_to_all(parts, ("y", "z"), 0, 0, tiled=True)
    mine, give = pl.pallas_call(
        finish_kernel,
        out_shape=[jax.ShapeDtypeStruct((here // 2, HD), BF16)] * 2,
        in_specs=[smem()] + [vmem()] * 4,
        out_specs=[vmem()] * 2,
        compiler_params=params,
    )(place, parts, new_key, new_value, other)
    result = pl.pallas_call(
        join_kernel,
        out_shape=jax.ShapeDtypeStruct((depths, here, HD), BF16),
        in_specs=[smem(), vmem(), vmem()],
        out_specs=vmem(),
        compiler_params=params,
    )(place, mine, shift(give, "c", 1))
    result = lax.all_to_all(result, "z", 0, 0, tiled=True)
    result = [result] + [shift(result, "x", k) for k in range(1, quarters)]
    return pl.pallas_call(
        place_kernel,
        out_shape=jax.ShapeDtypeStruct((rows, owners * QPG * HD), BF16),
        in_specs=[smem()] + [vmem()] * quarters,
        out_specs=vmem(),
        scratch_shapes=[pltpu.VMEM((quarters, depths, here, HD), BF16)],
        compiler_params=params,
    )(place, *result)


def solution(mesh):
    sizes = (8, 4, 4, 2)
    mesh = Mesh(mesh.devices.reshape(sizes), ("z", "x", "y", "c"))
    kv, req = ("z", "x"), ("y", "c")
    return jax.shard_map(
        per_device,
        mesh=mesh,
        in_specs=(
            P(req, kv),
            P(kv, None),
            P(req, None),
            P(req, None),
            P(req, kv, None),
            P(req, kv, None),
            P(),
            P(),
            P(kv),
            P(kv),
        ),
        out_specs=P(req, None),
        check_vma=False,
    )
```

```python
import functools

import jax
import jax.numpy as jnp
from jax import lax
from jax.experimental import pallas as pl
from jax.experimental.pallas import tpu as pltpu
from jax.sharding import Mesh
from jax.sharding import PartitionSpec as P

HD = 128
QPG = 8
BLOCK = 512
DOCS = 24
CHUNK = 16
ROWS = CHUNK * QPG
TOGETHER = 8
PIECES = 3
HALF = HD // 2
MOST = 16
LOG2E = 1.4426950408889634

NEG = -1e30
F32 = jnp.float32
BF16 = jnp.bfloat16
VMEM_BYTES = 16 * 1024 * 1024


def dot(a, b):
    return jnp.dot(a, b, preferred_element_type=F32)


def iota(shape, axis):
    return lax.broadcasted_iota(jnp.int32, shape, axis)


def vmem():
    return pl.BlockSpec(memory_space=pltpu.VMEM)


def smem():
    return pl.BlockSpec(memory_space=pltpu.SMEM)


def split(value):
    pieces = []
    for _ in range(PIECES):
        piece = value.astype(BF16).astype(F32)
        pieces.append(piece)
        value = value - piece
    return pieces


def plan_kernel(
    meta_ref, doc_col_ref, doc_row_ref, list_ref, sort_ref, unsort_ref, match_ref, *, slots
):
    count = doc_col_ref.shape[0]
    chunks = count // CHUNK
    found = 0
    for s in range(slots):

        def put(c, n, s=s):
            list_ref[n] = s * chunks + c
            return n + 1

        found = lax.fori_loop(meta_ref[slots + s], meta_ref[2 * slots + s], put, found)
    for u in range(TOGETHER):
        list_ref[found + u] = 0
    list_ref[slots * chunks + TOGETHER] = found

    col = doc_col_ref[:, :1]
    row = doc_row_ref[:1, :]
    down, across = iota((count, count), 0), iota((count, count), 1)
    before = jnp.where((col < row) | ((col == row) & (down < across)), 1.0, 0.0)
    rank_row = jnp.sum(before, axis=0, keepdims=True).astype(jnp.int32)
    behind = jnp.where((row < col) | ((row == col) & (across < down)), 1.0, 0.0)
    rank_col = jnp.sum(behind, axis=1, keepdims=True).astype(jnp.int32)
    unsort = jnp.where(across == rank_col, 1.0, 0.0).astype(BF16)
    sort_ref[...] = jnp.where(down == rank_row, 1.0, 0.0).astype(BF16)
    unsort_ref[...] = unsort
    docs = dot(doc_row_ref[...].astype(F32).astype(BF16), unsort)
    docs = jnp.concatenate([docs] * (MOST // 8), axis=0)
    docs = jnp.where(iota((MOST, count), 1) // CHUNK == iota((MOST, count), 0), docs, 0.0)
    same = iota((count, ROWS), 0) % CHUNK == iota((count, ROWS), 1) % CHUNK
    match_ref[...] = dot(docs.astype(BF16), jnp.where(same, 1.0, 0.0).astype(BF16))


def attend_kernel(meta_ref, list_ref, sort_ref, unsort_ref, d_ref, *refs):
    quarters = (len(refs) - 6) // 2
    query_refs, (key_ref, value_ref) = refs[:quarters], refs[quarters : quarters + 2]
    out_refs = refs[quarters + 2 : 2 * quarters + 2]
    q_ref, m_ref, l_ref, acc_ref = refs[2 * quarters + 2 :]
    count = sort_ref.shape[0]
    chunks = count // CHUNK
    slots = key_ref.shape[0] // BLOCK
    here = count // quarters
    scale = HD ** (-0.5)
    found = list_ref[slots * chunks + TOGETHER]
    sort, unsort = sort_ref[...], unsort_ref[...]
    for h in range(QPG):
        blocks = jnp.concatenate([ref[h, :, :] for ref in query_refs], axis=0)
        ordered = dot(sort, blocks).astype(BF16)
        for c in range(chunks):
            at = c * ROWS + h * CHUNK
            q_ref[at : at + CHUNK, :] = ordered[c * CHUNK : (c + 1) * CHUNK, :]
    m_ref[...] = jnp.full_like(m_ref, NEG)
    l_ref[...] = jnp.zeros_like(l_ref)
    acc_ref[...] = jnp.zeros_like(acc_ref)

    def some(step, _):
        local = []
        for u in range(TOGETHER):
            k = step * TOGETHER + u
            s, c = list_ref[k] // chunks, list_ref[k] % chunks
            doc = jnp.where(k < found, meta_ref[s], -1).astype(F32)
            rows = pl.ds(pl.multiple_of(c * ROWS, ROWS), ROWS)
            tokens = pl.ds(pl.multiple_of(s * BLOCK, BLOCK), BLOCK)
            scores = lax.dot_general(
                key_ref[tokens, :],
                q_ref[rows, :],
                (((1,), (1,)), ((), ())),
                preferred_element_type=F32,
            )
            alive = iota((BLOCK, ROWS), 0) < meta_ref[3 * slots + s]
            scores = jnp.where(alive, scores, NEG)
            top = jnp.max(scores, axis=0, keepdims=True)
            probs = jnp.exp2(scores * (scale * LOG2E) - top * (scale * LOG2E))
            top = top * scale
            total = jnp.sum(probs, axis=0, keepdims=True)
            mixed = dot(value_ref[:, tokens], probs.astype(BF16))
            local.append((c, doc, top, total, mixed))
        for c, doc, top, total, mixed in local:
            one = pl.ds(c, 1)
            match = d_ref[one, :] == doc
            old = m_ref[one, :]
            new = jnp.where(match, jnp.maximum(old, top), old)
            left = jnp.exp(old - new)
            right = jnp.where(match, jnp.exp(top - new), 0.0)
            m_ref[one, :] = new
            l_ref[one, :] = l_ref[one, :] * left + total * right
            acc_ref[c] = acc_ref[c] * left + mixed * right
        return 0

    lax.fori_loop(0, (found + TOGETHER - 1) // TOGETHER, some, 0)

    facts = jnp.concatenate([m_ref[...], l_ref[...]], axis=0)
    pad = jnp.zeros((HD - 2 * MOST * PIECES, ROWS), F32)
    facts = jnp.transpose(jnp.concatenate(split(facts) + [pad], axis=0)).astype(BF16)
    turned = [jnp.transpose(acc_ref[c]) for c in range(chunks)]
    lane = iota((count, HD), 1)
    mine = (lane % CHUNK == iota((count, HD), 0) // CHUNK) & (lane < 2 * MOST * PIECES)
    lane, column = iota((HD, HD), 0), iota((HD, HD), 1)
    blocks = []
    packed = jnp.zeros((count, HD), F32)
    for h in range(QPG):
        at = slice(h * CHUNK, (h + 1) * CHUNK)
        blocks.append(jnp.concatenate([block[at] for block in turned], axis=0))
        fact = jnp.concatenate([facts[at]] * chunks, axis=0)
        fact = jnp.where(mine, fact, jnp.zeros_like(fact))
        pick = jnp.where(lane // MOST * QPG + h == column, 1.0, 0.0).astype(BF16)
        packed = packed + dot(fact, pick)
    blocks.append(packed)
    for h, block in enumerate(blocks):
        block = dot(unsort, block.astype(BF16)).astype(BF16)
        for k in range(quarters):
            out_refs[k][h, :, :] = block[k * here : (k + 1) * here, :]


def spread_kernel(parts_ref, out_ref):
    copies, here, _ = out_ref.shape
    total = parts_ref[:, 0, :, :]
    for z in range(1, parts_ref.shape[1]):
        total = total + parts_ref[:, z, :, :]
    query = total.reshape(here, HD).astype(BF16)
    for k in range(copies):
        out_ref[k, :, :] = query


def merge_kernel(place_ref, query_ref, *refs):
    parts_refs, out_ref = refs[:-1], refs[-1]
    sources = len(parts_refs)
    _, here, _ = query_ref.shape
    wide = QPG * HD
    lanes, head = iota((HD, wide), 0), iota((HD, wide), 1) // HD
    known = lanes < 2 * QPG * PIECES
    pick_m = jnp.where((lanes % (2 * QPG) == head) & known, 1.0, 0.0).astype(BF16)
    pick_l = jnp.where((lanes % (2 * QPG) == head + QPG) & known, 1.0, 0.0).astype(BF16)
    facts = [ref[QPG, :, :] for ref in parts_refs]
    tops = [dot(fact, pick_m) for fact in facts]
    totals = [dot(fact, pick_l) for fact in facts]
    top = tops[0]
    for s in range(1, sources):
        top = jnp.maximum(top, tops[s])
    total = jnp.zeros((here, wide), F32)
    mixed = [jnp.zeros((here, HD), F32)] * QPG
    for s in range(sources):
        weight = jnp.exp(tops[s] - top)
        total = total + weight * totals[s]
        for h in range(QPG):
            part = parts_refs[s][h, :, :].astype(F32)
            mixed[h] = mixed[h] + weight[:, h * HD : (h + 1) * HD] * part
    lane = iota((here, HD), 1) % HALF
    z = place_ref[0]
    down, across = iota((HD, HD), 0), iota((HD, HD), 1) % HALF
    pick = jnp.where((across < 16) & (down == 16 * z + across), 1.0, 0.0).astype(BF16)
    left = iota((8, HD), 1) < HALF
    for h in range(QPG):
        fact = dot(query_ref[h, :, :], pick)
        pieces = split(top[:, h * HD : (h + 1) * HD]) + split(total[:, h * HD : (h + 1) * HD])
        for k, piece in enumerate(pieces):
            fact = jnp.where(lane == 16 + k, piece, fact)
        for y in range(here // 16):
            at = 16 * y
            facts = jnp.where(left, fact[at : at + 8], fact[at + 8 : at + 16])
            tile = jnp.concatenate([mixed[h][at : at + 16], facts], axis=0)
            out_ref[y * QPG + h, :, :] = tile.astype(BF16)


def finish_kernel(place_ref, parts_ref, key_ref, value_ref, other_ref, mine_ref, give_ref):
    depths, rows = QPG, key_ref.shape[0]
    lines = parts_ref.shape[0] // depths
    x, c = place_ref[1], place_ref[2]
    pick = jnp.where(iota((8, rows), 1) == iota((8, rows), 0) + 8 * x, 1.0, 0.0).astype(BF16)
    own = [dot(pick, ref[...]) for ref in (key_ref, value_ref)]
    other = [dot(pick, other_ref[k * rows : (k + 1) * rows, :]) for k in range(2)]
    lanes, column = iota((HD, 4 * HD), 0), iota((HD, 4 * HD), 1)
    low = column // (2 * HD) * HALF + 16 + column // HD % 2 * PIECES
    pick = jnp.where((lanes >= low) & (lanes < low + PIECES), 1.0, 0.0).astype(BF16)
    facts, spread = [], []
    for z in range(depths):
        fact = jnp.concatenate(
            [parts_ref[y * depths + z, :, :].astype(F32)[16:] for y in range(lines)], axis=0
        )
        facts.append(fact)
        spread.append(dot(fact.astype(BF16), pick))
    lane = iota((8 * lines, HD), 1) // 16
    mine, give = [], []
    queries = []
    for e in range(2):
        query = jnp.zeros((8 * lines, HD), F32)
        for z in range(depths):
            turned = pltpu.roll(facts[z], (16 * z - HALF * e) % HD, 1)
            query = jnp.where(lane == z, turned, query)
        queries.append(query)
    for y in range(lines):
        at = slice(8 * y, 8 * y + 8)
        done = []
        for e in range(2):
            key, value = [
                jnp.where(
                    c == 0,
                    block[:, 2 * y * HD : (2 * y + 1) * HD],
                    block[:, (2 * y + 1) * HD : (2 * y + 2) * HD],
                )
                for block in [jnp.where(c == e, a, b) for a, b in zip(own, other)]
            ]
            score = jnp.sum(queries[e][at] * key, axis=1, keepdims=True) * (HD ** (-0.5))
            score = jnp.broadcast_to(score, (8, HD))
            tops = [block[at, 2 * e * HD : (2 * e + 1) * HD] for block in spread]
            totals = [block[at, (2 * e + 1) * HD : (2 * e + 2) * HD] for block in spread]
            top = score
            for z in range(depths):
                top = jnp.maximum(top, tops[z])
            total = jnp.exp(score - top)
            mixed = total * value
            for z in range(depths):
                weight = jnp.exp(tops[z] - top)
                total = total + weight * totals[z]
                part = parts_ref[y * depths + z, :, :].astype(F32)[8 * e : 8 * e + 8]
                mixed = mixed + weight * part
            done.append(mixed / total)
        mine.append(jnp.where(c == 0, done[0], done[1]))
        give.append(jnp.where(c == 0, done[1], done[0]))
    mine_ref[...] = jnp.concatenate(mine, axis=0).astype(BF16)
    give_ref[...] = jnp.concatenate(give, axis=0).astype(BF16)


def join_kernel(place_ref, mine_ref, got_ref, out_ref):
    c = place_ref[2]
    mine, got = mine_ref[...].astype(F32), got_ref[...].astype(F32)
    first, second = jnp.where(c == 0, mine, got), jnp.where(c == 0, got, mine)
    rows = []
    for y in range(mine.shape[0] // 8):
        at = slice(8 * y, 8 * y + 8)
        rows += [first[at], second[at]]
    joined = jnp.concatenate(rows, axis=0).astype(BF16)
    for k in range(out_ref.shape[0]):
        out_ref[k, :, :] = joined


def place_kernel(place_ref, *refs):
    blocks, out_ref, held_ref = refs[:-2], refs[-2], refs[-1]
    quarters = len(blocks)
    depths, here, _ = blocks[0].shape
    x = place_ref[1]
    for k, ref in enumerate(blocks):
        held_ref[(x + quarters - k) % quarters] = ref[...]
    for x in range(0, quarters, 2):
        for z in range(depths):
            first = held_ref[x, z, :, :].astype(F32)
            second = held_ref[x + 1, z, :, :].astype(F32)
            for i in range(here // 8):
                rows = slice(8 * i, 8 * i + 8)
                at = (i * depths + z) * HD
                out_ref[8 * x : 8 * x + 16, at : at + HD] = jnp.concatenate(
                    [first[rows], second[rows]], axis=0
                ).astype(BF16)


def plan_call(meta, doc_col, doc_row, slots):
    count = doc_col.shape[0]
    chunks = count // CHUNK
    return pl.pallas_call(
        functools.partial(plan_kernel, slots=slots),
        out_shape=[
            jax.ShapeDtypeStruct((slots * chunks + TOGETHER + 1,), jnp.int32),
            jax.ShapeDtypeStruct((count, count), BF16),
            jax.ShapeDtypeStruct((count, count), BF16),
            jax.ShapeDtypeStruct((MOST, ROWS), F32),
        ],
        in_specs=[smem(), vmem(), vmem()],
        out_specs=[smem(), vmem(), vmem(), vmem()],
        compiler_params=pltpu.CompilerParams(vmem_limit_bytes=VMEM_BYTES),
        cost_estimate=pl.CostEstimate(
            flops=2 * count**3, bytes_accessed=8 * count * count, transcendentals=0
        ),
    )(meta, doc_col, doc_row)


def attend_call(meta, plan, queries, keys, values):
    quarters = len(queries)
    here = queries[0].shape[1]
    count = quarters * here
    slots = keys.shape[0] // BLOCK
    return pl.pallas_call(
        attend_kernel,
        out_shape=[jax.ShapeDtypeStruct((QPG + 1, here, HD), BF16)] * quarters,
        in_specs=[smem(), smem()] + [vmem()] * (5 + quarters),
        out_specs=[vmem()] * quarters,
        scratch_shapes=[
            pltpu.VMEM((count * QPG, HD), BF16),
            pltpu.VMEM((MOST, ROWS), F32),
            pltpu.VMEM((MOST, ROWS), F32),
            pltpu.VMEM((count // CHUNK, HD, ROWS), F32),
        ],
        compiler_params=pltpu.CompilerParams(vmem_limit_bytes=VMEM_BYTES),
        cost_estimate=pl.CostEstimate(
            flops=count * QPG * BLOCK * slots * HD * 4, bytes_accessed=4 * 2**20, transcendentals=0
        ),
    )(meta, *plan, *queries, keys, values)


def shift(block, axis, step):
    size = lax.axis_size(axis)
    return lax.ppermute(block, axis, [(i, (i + step) % size) for i in range(size)])


def per_device(
    hidden,
    q_weight,
    new_key,
    new_value,
    key_cache,
    value_cache,
    req_doc,
    doc_len,
    slot_doc,
    slot_blk,
):
    depths, quarters = lax.axis_size("z"), lax.axis_size("x")
    owners = lax.axis_size("y") * lax.axis_size("c")
    rows = hidden.shape[0]
    count = owners * rows
    here = count // quarters
    slots = slot_doc.shape[0]
    z, x = lax.axis_index("z"), lax.axis_index("x")
    place = jnp.stack([z, x, lax.axis_index("c")])

    docs = req_doc.reshape(owners, quarters, rows // quarters).transpose(1, 0, 2)
    docs = docs[(x - jnp.arange(quarters)) % quarters].reshape(count)
    doc_ids = jnp.arange(DOCS)
    slot_len = jnp.sum(
        jnp.where(slot_doc[:, None] == doc_ids[None, :], doc_len[None, :], 0), axis=1
    )
    remain = jnp.clip(slot_len - slot_blk * BLOCK, 0, BLOCK)

    def layout(docs):
        size = docs.shape[0]
        lower = jnp.sum((docs[None, :] < slot_doc[:, None]).astype(jnp.int32), axis=1)
        upper = jnp.sum((docs[None, :] <= slot_doc[:, None]).astype(jnp.int32), axis=1)
        first = lower // CHUNK
        last = jnp.where((upper > lower) & (remain > 0), (upper + CHUNK - 1) // CHUNK, first)
        meta = jnp.concatenate([slot_doc, first, last, remain])
        doc_col = jnp.broadcast_to(docs[:, None], (size, HD))
        doc_row = jnp.broadcast_to(docs[None, :], (8, size))
        return meta, plan_call(meta, doc_col, doc_row, slots)

    params = pltpu.CompilerParams(vmem_limit_bytes=VMEM_BYTES)
    plans = (layout(docs[:here]), layout(docs[here:]))
    partial = dot(hidden, q_weight).astype(jnp.float16)
    partial = [
        lax.dynamic_slice_in_dim(partial, (x + k) % quarters * 8, 8, 0) for k in range(quarters)
    ]
    partial = [partial[0]] + [shift(partial[k], "x", k) for k in range(1, quarters)]
    partial = sum(block.astype(F32) for block in partial).astype(jnp.float16)
    partial, plans = lax.optimization_barrier((partial, plans))
    partial = partial.reshape(8, owners * QPG, HD).transpose(1, 0, 2)
    partial = lax.all_to_all(partial, ("y", "c", "z"), 0, 0, tiled=True)
    query = pl.pallas_call(
        spread_kernel,
        out_shape=jax.ShapeDtypeStruct((depths, here, HD), BF16),
        in_specs=[vmem()],
        out_specs=vmem(),
        compiler_params=params,
    )(partial.reshape(owners, depths, 8, HD).astype(F32))
    query = lax.all_to_all(query, "z", 0, 0, tiled=True)
    queries = [query] + [shift(query, "x", k) for k in range(1, quarters)]
    values = value_cache[0].T
    parts = [
        *attend_call(*plans[0], queries[:1], key_cache[0], values),
        *attend_call(*plans[1], queries[1:], key_cache[0], values),
    ]
    parts = [parts[-k % quarters] for k in range(quarters)]
    parts = [parts[0]] + [shift(parts[k], "x", k) for k in range(1, quarters)]
    other = shift(jnp.concatenate([new_key, new_value], axis=0), "c", 1)
    parts, other = lax.optimization_barrier((parts, other))
    parts = pl.pallas_call(
        merge_kernel,
        out_shape=jax.ShapeDtypeStruct((owners // 2 * QPG, 24, HD), BF16),
        in_specs=[smem()] + [vmem()] * (quarters + 1),
        out_specs=vmem(),
        compiler_params=params,
    )(place, query, *parts)
    parts = lax.all_to_all(parts, ("y", "z"), 0, 0, tiled=True)
    mine, give = pl.pallas_call(
        finish_kernel,
        out_shape=[jax.ShapeDtypeStruct((here // 2, HD), BF16)] * 2,
        in_specs=[smem()] + [vmem()] * 4,
        out_specs=[vmem()] * 2,
        compiler_params=params,
    )(place, parts, new_key, new_value, other)
    result = pl.pallas_call(
        join_kernel,
        out_shape=jax.ShapeDtypeStruct((depths, here, HD), BF16),
        in_specs=[smem(), vmem(), vmem()],
        out_specs=vmem(),
        compiler_params=params,
    )(place, mine, shift(give, "c", 1))
    result = lax.all_to_all(result, "z", 0, 0, tiled=True)
    result = [result] + [shift(result, "x", k) for k in range(1, quarters)]
    return pl.pallas_call(
        place_kernel,
        out_shape=jax.ShapeDtypeStruct((rows, owners * QPG * HD), BF16),
        in_specs=[smem()] + [vmem()] * quarters,
        out_specs=vmem(),
        scratch_shapes=[pltpu.VMEM((quarters, depths, here, HD), BF16)],
        compiler_params=params,
    )(place, *result)


def solution(mesh):
    sizes = (8, 4, 4, 2)
    mesh = Mesh(mesh.devices.reshape(sizes), ("z", "x", "y", "c"))
    kv, req = ("z", "x"), ("y", "c")
    return jax.shard_map(
        per_device,
        mesh=mesh,
        in_specs=(
            P(req, kv),
            P(kv, None),
            P(req, None),
            P(req, None),
            P(req, kv, None),
            P(req, kv, None),
            P(),
            P(),
            P(kv),
            P(kv),
        ),
        out_specs=P(req, None),
        check_vma=False,
    )
```

```python
import functools

import jax
import jax.numpy as jnp
from jax import lax
from jax.experimental import pallas as pl
from jax.experimental.pallas import tpu as pltpu
from jax.sharding import Mesh
from jax.sharding import PartitionSpec as P

HD = 128
QPG = 8
BLOCK = 512
DOCS = 24
CHUNK = 16
ROWS = CHUNK * QPG
TOGETHER = 8
PIECES = 3
HALF = HD // 2
MOST = 16
LOG2E = 1.4426950408889634

NEG = -1e30
F32 = jnp.float32
BF16 = jnp.bfloat16
VMEM_BYTES = 16 * 1024 * 1024


def dot(a, b):
    return jnp.dot(a, b, preferred_element_type=F32)


def iota(shape, axis):
    return lax.broadcasted_iota(jnp.int32, shape, axis)


def vmem():
    return pl.BlockSpec(memory_space=pltpu.VMEM)


def smem():
    return pl.BlockSpec(memory_space=pltpu.SMEM)


def split(value):
    pieces = []
    for _ in range(PIECES):
        piece = value.astype(BF16).astype(F32)
        pieces.append(piece)
        value = value - piece
    return pieces


def plan_kernel(
    meta_ref, doc_col_ref, doc_row_ref, list_ref, sort_ref, unsort_ref, match_ref, *, slots
):
    count = doc_col_ref.shape[0]
    chunks = count // CHUNK
    found = 0
    for s in range(slots):

        def put(c, n, s=s):
            list_ref[n] = s * chunks + c
            return n + 1

        found = lax.fori_loop(meta_ref[slots + s], meta_ref[2 * slots + s], put, found)
    for u in range(TOGETHER):
        list_ref[found + u] = 0
    list_ref[slots * chunks + TOGETHER] = found

    col = doc_col_ref[:, :1]
    row = doc_row_ref[:1, :]
    down, across = iota((count, count), 0), iota((count, count), 1)
    before = jnp.where((col < row) | ((col == row) & (down < across)), 1.0, 0.0)
    rank_row = jnp.sum(before, axis=0, keepdims=True).astype(jnp.int32)
    behind = jnp.where((row < col) | ((row == col) & (across < down)), 1.0, 0.0)
    rank_col = jnp.sum(behind, axis=1, keepdims=True).astype(jnp.int32)
    unsort = jnp.where(across == rank_col, 1.0, 0.0).astype(BF16)
    sort_ref[...] = jnp.where(down == rank_row, 1.0, 0.0).astype(BF16)
    unsort_ref[...] = unsort
    docs = dot(doc_row_ref[...].astype(F32).astype(BF16), unsort)
    docs = jnp.concatenate([docs] * (MOST // 8), axis=0)
    docs = jnp.where(iota((MOST, count), 1) // CHUNK == iota((MOST, count), 0), docs, 0.0)
    same = iota((count, ROWS), 0) % CHUNK == iota((count, ROWS), 1) % CHUNK
    match_ref[...] = dot(docs.astype(BF16), jnp.where(same, 1.0, 0.0).astype(BF16))


def attend_kernel(meta_ref, list_ref, sort_ref, unsort_ref, d_ref, *refs):
    quarters = (len(refs) - 6) // 2
    query_refs, (key_ref, value_ref) = refs[:quarters], refs[quarters : quarters + 2]
    out_refs = refs[quarters + 2 : 2 * quarters + 2]
    q_ref, m_ref, l_ref, acc_ref = refs[2 * quarters + 2 :]
    count = sort_ref.shape[0]
    chunks = count // CHUNK
    slots = key_ref.shape[0] // BLOCK
    here = count // quarters
    scale = HD ** (-0.5)
    found = list_ref[slots * chunks + TOGETHER]
    sort, unsort = sort_ref[...], unsort_ref[...]
    for h in range(QPG):
        blocks = jnp.concatenate([ref[h, :, :] for ref in query_refs], axis=0)
        ordered = dot(sort, blocks).astype(BF16)
        for c in range(chunks):
            at = c * ROWS + h * CHUNK
            q_ref[at : at + CHUNK, :] = ordered[c * CHUNK : (c + 1) * CHUNK, :]
    m_ref[...] = jnp.full_like(m_ref, NEG)
    l_ref[...] = jnp.zeros_like(l_ref)
    acc_ref[...] = jnp.zeros_like(acc_ref)

    def some(start, width):
        local = []
        for u in range(width):
            k = start + u
            s, c = list_ref[k] // chunks, list_ref[k] % chunks
            doc = jnp.where(k < found, meta_ref[s], -1).astype(F32)
            rows = pl.ds(pl.multiple_of(c * ROWS, ROWS), ROWS)
            tokens = pl.ds(pl.multiple_of(s * BLOCK, BLOCK), BLOCK)
            scores = lax.dot_general(
                key_ref[tokens, :],
                q_ref[rows, :],
                (((1,), (1,)), ((), ())),
                preferred_element_type=F32,
            )
            alive = iota((BLOCK, ROWS), 0) < meta_ref[3 * slots + s]
            scores = jnp.where(alive, scores, NEG)
            top = jnp.max(scores, axis=0, keepdims=True)
            probs = jnp.exp2(scores * (scale * LOG2E) - top * (scale * LOG2E))
            top = top * scale
            total = jnp.sum(probs, axis=0, keepdims=True)
            mixed = dot(value_ref[:, tokens], probs.astype(BF16))
            local.append((c, doc, top, total, mixed))
        for c, doc, top, total, mixed in local:
            one = pl.ds(c, 1)
            match = d_ref[one, :] == doc
            old = m_ref[one, :]
            new = jnp.where(match, jnp.maximum(old, top), old)
            left = jnp.exp(old - new)
            right = jnp.where(match, jnp.exp(top - new), 0.0)
            m_ref[one, :] = new
            l_ref[one, :] = l_ref[one, :] * left + total * right
            acc_ref[c] = acc_ref[c] * left + mixed * right
        return 0

    half = TOGETHER // 2
    whole = (found + half - 1) // TOGETHER
    rest = (found - whole * TOGETHER + half - 1) // half
    lax.fori_loop(0, whole, lambda k, _: some(k * TOGETHER, TOGETHER), 0)
    lax.fori_loop(0, rest, lambda k, _: some(whole * TOGETHER + k * half, half), 0)

    facts = jnp.concatenate([m_ref[...], l_ref[...]], axis=0)
    pad = jnp.zeros((HD - 2 * MOST * PIECES, ROWS), F32)
    facts = jnp.transpose(jnp.concatenate(split(facts) + [pad], axis=0)).astype(BF16)
    turned = [jnp.transpose(acc_ref[c]) for c in range(chunks)]
    lane = iota((count, HD), 1)
    mine = (lane % CHUNK == iota((count, HD), 0) // CHUNK) & (lane < 2 * MOST * PIECES)
    lane, column = iota((HD, HD), 0), iota((HD, HD), 1)
    blocks = []
    packed = jnp.zeros((count, HD), F32)
    for h in range(QPG):
        at = slice(h * CHUNK, (h + 1) * CHUNK)
        blocks.append(jnp.concatenate([block[at] for block in turned], axis=0))
        fact = jnp.concatenate([facts[at]] * chunks, axis=0)
        fact = jnp.where(mine, fact, jnp.zeros_like(fact))
        pick = jnp.where(lane // MOST * QPG + h == column, 1.0, 0.0).astype(BF16)
        packed = packed + dot(fact, pick)
    blocks.append(packed)
    for h, block in enumerate(blocks):
        block = dot(unsort, block.astype(BF16)).astype(BF16)
        for k in range(quarters):
            out_refs[k][h, :, :] = block[k * here : (k + 1) * here, :]


def spread_kernel(parts_ref, out_ref):
    copies, here, _ = out_ref.shape
    total = parts_ref[:, 0, :, :]
    for z in range(1, parts_ref.shape[1]):
        total = total + parts_ref[:, z, :, :]
    query = total.reshape(here, HD).astype(BF16)
    for k in range(copies):
        out_ref[k, :, :] = query


def merge_kernel(place_ref, query_ref, *refs):
    parts_refs, out_ref = refs[:-1], refs[-1]
    sources = len(parts_refs)
    _, here, _ = query_ref.shape
    wide = QPG * HD
    lanes, head = iota((HD, wide), 0), iota((HD, wide), 1) // HD
    known = lanes < 2 * QPG * PIECES
    pick_m = jnp.where((lanes % (2 * QPG) == head) & known, 1.0, 0.0).astype(BF16)
    pick_l = jnp.where((lanes % (2 * QPG) == head + QPG) & known, 1.0, 0.0).astype(BF16)
    facts = [ref[QPG, :, :] for ref in parts_refs]
    tops = [dot(fact, pick_m) for fact in facts]
    totals = [dot(fact, pick_l) for fact in facts]
    top = tops[0]
    for s in range(1, sources):
        top = jnp.maximum(top, tops[s])
    total = jnp.zeros((here, wide), F32)
    mixed = [jnp.zeros((here, HD), F32)] * QPG
    for s in range(sources):
        weight = jnp.exp(tops[s] - top)
        total = total + weight * totals[s]
        for h in range(QPG):
            part = parts_refs[s][h, :, :].astype(F32)
            mixed[h] = mixed[h] + weight[:, h * HD : (h + 1) * HD] * part
    lane = iota((here, HD), 1) % HALF
    z = place_ref[0]
    down, across = iota((HD, HD), 0), iota((HD, HD), 1) % HALF
    pick = jnp.where((across < 16) & (down == 16 * z + across), 1.0, 0.0).astype(BF16)
    left = iota((8, HD), 1) < HALF
    for h in range(QPG):
        fact = dot(query_ref[h, :, :], pick)
        pieces = split(top[:, h * HD : (h + 1) * HD]) + split(total[:, h * HD : (h + 1) * HD])
        for k, piece in enumerate(pieces):
            fact = jnp.where(lane == 16 + k, piece, fact)
        for y in range(here // 16):
            at = 16 * y
            facts = jnp.where(left, fact[at : at + 8], fact[at + 8 : at + 16])
            tile = jnp.concatenate([mixed[h][at : at + 16], facts], axis=0)
            out_ref[y * QPG + h, :, :] = tile.astype(BF16)


def finish_kernel(place_ref, parts_ref, key_ref, value_ref, other_ref, mine_ref, give_ref):
    depths, rows = QPG, key_ref.shape[0]
    lines = parts_ref.shape[0] // depths
    x, c = place_ref[1], place_ref[2]
    pick = jnp.where(iota((8, rows), 1) == iota((8, rows), 0) + 8 * x, 1.0, 0.0).astype(BF16)
    own = [dot(pick, ref[...]) for ref in (key_ref, value_ref)]
    other = [dot(pick, other_ref[k * rows : (k + 1) * rows, :]) for k in range(2)]
    lanes, column = iota((HD, 4 * HD), 0), iota((HD, 4 * HD), 1)
    low = column // (2 * HD) * HALF + 16 + column // HD % 2 * PIECES
    pick = jnp.where((lanes >= low) & (lanes < low + PIECES), 1.0, 0.0).astype(BF16)
    facts, spread = [], []
    for z in range(depths):
        fact = jnp.concatenate(
            [parts_ref[y * depths + z, :, :].astype(F32)[16:] for y in range(lines)], axis=0
        )
        facts.append(fact)
        spread.append(dot(fact.astype(BF16), pick))
    lane = iota((8 * lines, HD), 1) // 16
    mine, give = [], []
    queries = []
    for e in range(2):
        query = jnp.zeros((8 * lines, HD), F32)
        for z in range(depths):
            turned = pltpu.roll(facts[z], (16 * z - HALF * e) % HD, 1)
            query = jnp.where(lane == z, turned, query)
        queries.append(query)
    for y in range(lines):
        at = slice(8 * y, 8 * y + 8)
        done = []
        for e in range(2):
            key, value = [
                jnp.where(
                    c == 0,
                    block[:, 2 * y * HD : (2 * y + 1) * HD],
                    block[:, (2 * y + 1) * HD : (2 * y + 2) * HD],
                )
                for block in [jnp.where(c == e, a, b) for a, b in zip(own, other)]
            ]
            score = jnp.sum(queries[e][at] * key, axis=1, keepdims=True) * (HD ** (-0.5))
            score = jnp.broadcast_to(score, (8, HD))
            tops = [block[at, 2 * e * HD : (2 * e + 1) * HD] for block in spread]
            totals = [block[at, (2 * e + 1) * HD : (2 * e + 2) * HD] for block in spread]
            top = score
            for z in range(depths):
                top = jnp.maximum(top, tops[z])
            total = jnp.exp(score - top)
            mixed = total * value
            for z in range(depths):
                weight = jnp.exp(tops[z] - top)
                total = total + weight * totals[z]
                part = parts_ref[y * depths + z, :, :].astype(F32)[8 * e : 8 * e + 8]
                mixed = mixed + weight * part
            done.append(mixed / total)
        mine.append(jnp.where(c == 0, done[0], done[1]))
        give.append(jnp.where(c == 0, done[1], done[0]))
    mine_ref[...] = jnp.concatenate(mine, axis=0).astype(BF16)
    give_ref[...] = jnp.concatenate(give, axis=0).astype(BF16)


def join_kernel(place_ref, mine_ref, got_ref, out_ref):
    c = place_ref[2]
    mine, got = mine_ref[...].astype(F32), got_ref[...].astype(F32)
    first, second = jnp.where(c == 0, mine, got), jnp.where(c == 0, got, mine)
    rows = []
    for y in range(mine.shape[0] // 8):
        at = slice(8 * y, 8 * y + 8)
        rows += [first[at], second[at]]
    joined = jnp.concatenate(rows, axis=0).astype(BF16)
    for k in range(out_ref.shape[0]):
        out_ref[k, :, :] = joined


def place_kernel(place_ref, *refs):
    blocks, out_ref, held_ref = refs[:-2], refs[-2], refs[-1]
    quarters = len(blocks)
    depths, here, _ = blocks[0].shape
    x = place_ref[1]
    for k, ref in enumerate(blocks):
        held_ref[(x + quarters - k) % quarters] = ref[...]
    for x in range(0, quarters, 2):
        for z in range(depths):
            first = held_ref[x, z, :, :].astype(F32)
            second = held_ref[x + 1, z, :, :].astype(F32)
            for i in range(here // 8):
                rows = slice(8 * i, 8 * i + 8)
                at = (i * depths + z) * HD
                out_ref[8 * x : 8 * x + 16, at : at + HD] = jnp.concatenate(
                    [first[rows], second[rows]], axis=0
                ).astype(BF16)


def plan_call(meta, doc_col, doc_row, slots):
    count = doc_col.shape[0]
    chunks = count // CHUNK
    return pl.pallas_call(
        functools.partial(plan_kernel, slots=slots),
        out_shape=[
            jax.ShapeDtypeStruct((slots * chunks + TOGETHER + 1,), jnp.int32),
            jax.ShapeDtypeStruct((count, count), BF16),
            jax.ShapeDtypeStruct((count, count), BF16),
            jax.ShapeDtypeStruct((MOST, ROWS), F32),
        ],
        in_specs=[smem(), vmem(), vmem()],
        out_specs=[smem(), vmem(), vmem(), vmem()],
        compiler_params=pltpu.CompilerParams(vmem_limit_bytes=VMEM_BYTES),
        cost_estimate=pl.CostEstimate(
            flops=2 * count**3, bytes_accessed=8 * count * count, transcendentals=0
        ),
    )(meta, doc_col, doc_row)


def attend_call(meta, plan, queries, keys, values):
    quarters = len(queries)
    here = queries[0].shape[1]
    count = quarters * here
    slots = keys.shape[0] // BLOCK
    return pl.pallas_call(
        attend_kernel,
        out_shape=[jax.ShapeDtypeStruct((QPG + 1, here, HD), BF16)] * quarters,
        in_specs=[smem(), smem()] + [vmem()] * (5 + quarters),
        out_specs=[vmem()] * quarters,
        scratch_shapes=[
            pltpu.VMEM((count * QPG, HD), BF16),
            pltpu.VMEM((MOST, ROWS), F32),
            pltpu.VMEM((MOST, ROWS), F32),
            pltpu.VMEM((count // CHUNK, HD, ROWS), F32),
        ],
        compiler_params=pltpu.CompilerParams(vmem_limit_bytes=VMEM_BYTES),
        cost_estimate=pl.CostEstimate(
            flops=count * QPG * BLOCK * slots * HD * 4, bytes_accessed=4 * 2**20, transcendentals=0
        ),
    )(meta, *plan, *queries, keys, values)


def shift(block, axis, step):
    size = lax.axis_size(axis)
    return lax.ppermute(block, axis, [(i, (i + step) % size) for i in range(size)])


def per_device(
    hidden,
    q_weight,
    new_key,
    new_value,
    key_cache,
    value_cache,
    req_doc,
    doc_len,
    slot_doc,
    slot_blk,
):
    depths, quarters = lax.axis_size("z"), lax.axis_size("x")
    owners = lax.axis_size("y") * lax.axis_size("c")
    rows = hidden.shape[0]
    count = owners * rows
    here = count // quarters
    slots = slot_doc.shape[0]
    z, x = lax.axis_index("z"), lax.axis_index("x")
    place = jnp.stack([z, x, lax.axis_index("c")])

    docs = req_doc.reshape(owners, quarters, rows // quarters).transpose(1, 0, 2)
    docs = docs[(x - jnp.arange(quarters)) % quarters].reshape(count)
    doc_ids = jnp.arange(DOCS)
    slot_len = jnp.sum(
        jnp.where(slot_doc[:, None] == doc_ids[None, :], doc_len[None, :], 0), axis=1
    )
    remain = jnp.clip(slot_len - slot_blk * BLOCK, 0, BLOCK)

    def layout(docs):
        size = docs.shape[0]
        lower = jnp.sum((docs[None, :] < slot_doc[:, None]).astype(jnp.int32), axis=1)
        upper = jnp.sum((docs[None, :] <= slot_doc[:, None]).astype(jnp.int32), axis=1)
        first = lower // CHUNK
        last = jnp.where((upper > lower) & (remain > 0), (upper + CHUNK - 1) // CHUNK, first)
        meta = jnp.concatenate([slot_doc, first, last, remain])
        doc_col = jnp.broadcast_to(docs[:, None], (size, HD))
        doc_row = jnp.broadcast_to(docs[None, :], (8, size))
        return meta, plan_call(meta, doc_col, doc_row, slots)

    params = pltpu.CompilerParams(vmem_limit_bytes=VMEM_BYTES)
    plans = (layout(docs[:here]), layout(docs[here:]))
    partial = dot(hidden, q_weight).astype(jnp.float16)
    partial = [
        lax.dynamic_slice_in_dim(partial, (x + k) % quarters * 8, 8, 0) for k in range(quarters)
    ]
    partial = [partial[0]] + [shift(partial[k], "x", k) for k in range(1, quarters)]
    partial = sum(block.astype(F32) for block in partial).astype(jnp.float16)
    partial, plans = lax.optimization_barrier((partial, plans))
    partial = partial.reshape(8, owners * QPG, HD).transpose(1, 0, 2)
    partial = lax.all_to_all(partial, ("y", "c", "z"), 0, 0, tiled=True)
    query = pl.pallas_call(
        spread_kernel,
        out_shape=jax.ShapeDtypeStruct((depths, here, HD), BF16),
        in_specs=[vmem()],
        out_specs=vmem(),
        compiler_params=params,
    )(partial.reshape(owners, depths, 8, HD).astype(F32))
    query = lax.all_to_all(query, "z", 0, 0, tiled=True)
    queries = [query] + [shift(query, "x", k) for k in range(1, quarters)]
    values = value_cache[0].T
    parts = [
        *attend_call(*plans[0], queries[:1], key_cache[0], values),
        *attend_call(*plans[1], queries[1:], key_cache[0], values),
    ]
    parts = [parts[-k % quarters] for k in range(quarters)]
    parts = [parts[0]] + [shift(parts[k], "x", k) for k in range(1, quarters)]
    other = shift(jnp.concatenate([new_key, new_value], axis=0), "c", 1)
    parts, other = lax.optimization_barrier((parts, other))
    parts = pl.pallas_call(
        merge_kernel,
        out_shape=jax.ShapeDtypeStruct((owners // 2 * QPG, 24, HD), BF16),
        in_specs=[smem()] + [vmem()] * (quarters + 1),
        out_specs=vmem(),
        compiler_params=params,
    )(place, query, *parts)
    parts = lax.all_to_all(parts, ("y", "z"), 0, 0, tiled=True)
    mine, give = pl.pallas_call(
        finish_kernel,
        out_shape=[jax.ShapeDtypeStruct((here // 2, HD), BF16)] * 2,
        in_specs=[smem()] + [vmem()] * 4,
        out_specs=[vmem()] * 2,
        compiler_params=params,
    )(place, parts, new_key, new_value, other)
    result = pl.pallas_call(
        join_kernel,
        out_shape=jax.ShapeDtypeStruct((depths, here, HD), BF16),
        in_specs=[smem(), vmem(), vmem()],
        out_specs=vmem(),
        compiler_params=params,
    )(place, mine, shift(give, "c", 1))
    result = lax.all_to_all(result, "z", 0, 0, tiled=True)
    result = [result] + [shift(result, "x", k) for k in range(1, quarters)]
    return pl.pallas_call(
        place_kernel,
        out_shape=jax.ShapeDtypeStruct((rows, owners * QPG * HD), BF16),
        in_specs=[smem()] + [vmem()] * quarters,
        out_specs=vmem(),
        scratch_shapes=[pltpu.VMEM((quarters, depths, here, HD), BF16)],
        compiler_params=params,
    )(place, *result)


def solution(mesh):
    sizes = (8, 4, 4, 2)
    mesh = Mesh(mesh.devices.reshape(sizes), ("z", "x", "y", "c"))
    kv, req = ("z", "x"), ("y", "c")
    return jax.shard_map(
        per_device,
        mesh=mesh,
        in_specs=(
            P(req, kv),
            P(kv, None),
            P(req, None),
            P(req, None),
            P(req, kv, None),
            P(req, kv, None),
            P(),
            P(),
            P(kv),
            P(kv),
        ),
        out_specs=P(req, None),
        check_vma=False,
    )
```
